256 devices in a mesh: seg: 8 (over y, core), coil: 16 (over x, z_lo), tile: 2 (over z_hi).
Axes of the slice: x: 4, y: 4, z: 8 (z_hi: 2, z_lo: 4; z = z_hi * 4 + z_lo), core: 2. Of those that a mesh axis runs over, the one named last changes fastest.
Arguments:
- right_side: float32 [1024, 128], P(('seg', 'coil', 'tile')), may hold values from -6 to 6
- sensitivity: float32 [32, 1024, 128], P('coil'), may hold values from -0.75 to 0.75
- field_map: float32 [1024, 64], replicated, may hold values from -12 to 12
- seg_map: int32 [1024, 4], replicated, may hold values from 0 to 23, all different within a row; in each aligned block of 1024 rows (0 to 1023, 1024 to 2047, ...) at most 256 rows name the same one
- sample_rows: int32 [24, 2048], P('seg', 'tile'), may hold values from 0 to 1023
- density: float32 [24, 2048, 64], P('seg', 'tile'), may hold values from 0.25 to 4
- step_alpha: float32 [2], replicated, may hold values from 0.15 to 0.35
- step_beta: float32 [2], replicated, may hold values from 0.1 to 0.5
Outputs:
- solution_field: float32 [1024, 128], P(('seg', 'coil', 'tile'))
- residual: float32 [1024, 128], P(('seg', 'coil', 'tile'))
The draws below stay inside these ranges and needn't reach their ends.
Inputs may be any that keep to these rules, and one draw needn't show every extreme that they name: `seg_map`: each row names 4 different segments; each segment is named by at most 256 tiles, a bound that some block reaches.
All inputs are finite; a program needn't handle non-finite values.
Results may differ from the reference program's by a relative error of at most 0.0001.
Values sent between devices are 32-bit elements; how exact they have to be, the bound alone decides.
No kernel may reach another device: no remote copies, remote signals or barrier semaphores. Data moves between devices by JAX's collectives and lax.ppermute only.
A program may use at most 128 MiB of HBM per device.

```python
import math
import jax
import jax.numpy as jnp
import numpy as np
from jax import lax

SEGS = 24
COILS = 32
TV = 64
TOP = 4
ITERS = 2
TILES = 1024
SROWS = 2048
CAP = 256


def set_ends(array, stream_key, least, top_value):
    spot = [jax.random.randint(jax.random.fold_in(stream_key, axis), (), 0, length) for axis, length in enumerate(array.shape)]
    main_axis = array.shape.index(max(array.shape))
    next_to = spot[:main_axis] + [(spot[main_axis] + 1) % array.shape[main_axis]] + spot[main_axis + 1:]
    return array.at[tuple(spot)].set(least).at[tuple(next_to)].set(top_value)


def block_levels(stream_key, shape, shards, least, largest):
    def one(position, parts):
        steps = jax.random.uniform(jax.random.fold_in(jax.random.fold_in(stream_key, 6), position), (parts,), jnp.float32, least / len(shards), largest / len(shards))
        return jnp.repeat(jnp.exp(steps), shape[position] // parts).reshape((-1,) + (1,) * (len(shape) - position - 1))

    loudness = one(*shards[0])
    for cut in shards[1:]:
        loudness = loudness * one(*cut)
    return loudness


def shared_out(own_key, own, number, rows, amount, top, limit, slope):
    ranking = jax.random.permutation(own_key, amount)
    heavy_load, common = portions_of(amount, rows * top, limit, slope, True), portions_of(amount, rows * top, limit, slope, False)
    places = jnp.arange(amount)

    def named(lengths, turn):
        used = int((lengths > 0).sum())
        fixed = max(1, used // 4)
        passed = fixed + (places - fixed + turn * (used - fixed)) % max(1, amount - fixed)
        return jnp.zeros((amount,), jnp.int32).at[ranking[jnp.where(places < fixed, places, passed)]].set(jnp.asarray(lengths, jnp.int32))

    lengths = jnp.where(number % 4 == 0, named(heavy_load, number // 4), named(common, number - number // 4 - 1))
    mixed = jax.random.permutation(jax.random.fold_in(own, 3), amount)
    source_of, receiver = mixed[0:amount // 2 * 2:2], mixed[1:amount // 2 * 2:2]
    room = jnp.minimum(lengths[source_of] - 1, limit - lengths[receiver]) // 2
    room = jnp.where((source_of == ranking[0]) | (receiver == ranking[0]) | (lengths[receiver] == 0), 0, jnp.maximum(room, 0))
    passed = jax.random.randint(jax.random.fold_in(own, 4), (amount // 2,), 0, 1 << 20) % (room + 1)
    lengths = lengths.at[source_of].add(-passed).at[receiver].add(passed)
    members = jnp.searchsorted(jnp.cumsum(lengths), jnp.arange(rows * top), side="right").astype(jnp.int32)
    table = members.reshape(top, rows).T
    table = table[jax.random.permutation(jax.random.fold_in(own, 1), rows)]
    turn = jax.random.randint(jax.random.fold_in(own, 2), (rows, 1), 0, top)
    return jnp.take_along_axis(table, (jnp.arange(top)[None, :] + turn) % top, axis=1)


def portions_of(count, total, reach, lean, full):
    loads = [(1 << 20) // math.isqrt(standing ** lean) + 1 for standing in range(1, count + 1)]
    largest = reach if full else min(reach, max(-(-total // count), total * loads[0] // sum(loads)))
    least = 1 if total - largest >= count - 1 else 0
    holding, surplus = [largest] + [least] * (count - 1), total - largest - least * (count - 1)
    while surplus > 0:
        movable = [i for i in range(1, count) if holding[i] < largest] or [i for i in range(1, count) if holding[i] < reach]
        mass, budget = sum([loads[i] for i in movable]), surplus
        for i in movable:
            extra = min(reach - holding[i], max(1, budget * loads[i] // mass), surplus)
            holding[i] = holding[i] + extra
            surplus = surplus - extra
    return np.array(holding)


def gaussian(rng, dims, scale, bound, shards=(), kind=jnp.bfloat16):
    gain = block_levels(rng, dims, shards, -0.22, 0.18) if shards else 1.0
    array = jax.random.normal(rng, dims, jnp.float32) * scale * gain
    return jnp.minimum(jnp.maximum(array, -bound), bound).astype(kind)


def setup_inputs(seed: int = 0) -> dict:
    streams_of = jax.random.split(jax.random.key(seed), 9)
    right_side = gaussian(streams_of[0], (TILES, 2 * TV), 1.0, 6.0, ((0, 256),), jnp.float32)
    sensitivity = gaussian(streams_of[1], (COILS, TILES, 2 * TV), 0.125, 0.75, ((0, 16),), jnp.float32)
    field_map = jnp.clip(jax.random.uniform(streams_of[2], (TILES, TV), jnp.float32, -12.0, 12.0), -12.0, 12.0)
    seg_map_keys = jax.random.split(jax.random.fold_in(streams_of[3], 1), TILES // TILES)
    seg_map_turns = jax.random.permutation(jax.random.fold_in(streams_of[3], 3), TILES // TILES)
    seg_map = jax.vmap(lambda own, number: shared_out(jax.random.fold_in(streams_of[3], 2), own, number, TILES, SEGS, TOP, CAP, 2))(seg_map_keys, seg_map_turns).reshape((TILES, TOP))
    sample_rows = set_ends(jax.random.randint(streams_of[4], (SEGS, SROWS), 0, TILES), jax.random.fold_in(streams_of[4], 1), 0, TILES - 1).astype(jnp.int32)
    density = jnp.clip(jnp.exp(math.log(4.0) - 2.7725887 * jax.random.uniform(streams_of[5], (SEGS, SROWS, TV), jnp.float32) ** block_levels(streams_of[5], (SEGS, SROWS, TV), ((0, 8), (1, 2)), -0.2, 0.2)), 0.25, 4.0)
    step_alpha = jnp.clip(jax.random.uniform(streams_of[6], (ITERS,), jnp.float32, 0.15, 0.35), 0.15, 0.35)
    step_beta = jnp.clip(jax.random.uniform(streams_of[7], (ITERS,), jnp.float32, 0.1, 0.5), 0.1, 0.5)
    return dict(right_side=right_side, sensitivity=sensitivity, field_map=field_map, seg_map=seg_map, sample_rows=sample_rows, density=density, step_alpha=step_alpha, step_beta=step_beta)


ridge_weight = 0.25
highest = lax.Precision.HIGHEST

def tile_list(seg_map, segment, slots):
    tile_count = seg_map.shape[0]
    is_member = jnp.any(seg_map == segment, axis=1).astype(jnp.int32)
    live_count = jnp.sum(is_member)
    sort_keys = (1 - is_member) * tile_count + jnp.arange(tile_count, dtype=jnp.int32)
    sorted_tiles = jnp.argsort(sort_keys).astype(jnp.int32)
    listed = sorted_tiles[:slots]
    valid_slots = (jnp.arange(slots, dtype=jnp.int32) < live_count).astype(jnp.float32)
    return (listed, valid_slots)

def row_tables(rows_here, listed, valid_slots, tile_count):
    product = rows_here[:, None] * listed[None, :] % tile_count
    angles = product.astype(jnp.float32) * jnp.float32(2.0 * math.pi / tile_count)
    slot_scale = valid_slots[None, :] / jnp.float32(math.sqrt(tile_count))
    return (jnp.cos(angles) * slot_scale, -jnp.sin(angles) * slot_scale)

def column_tables(voxels):
    steps_here = jnp.arange(voxels, dtype=jnp.int32)
    product = steps_here[:, None] * steps_here[None, :] % voxels
    angles = product.astype(jnp.float32) * jnp.float32(2.0 * math.pi / voxels)
    norm_factor = jnp.float32(1.0 / math.sqrt(voxels))
    return (jnp.cos(angles) * norm_factor, -jnp.sin(angles) * norm_factor)

def segment_normal(dir_rows, sens_rows, field_rows, seg_time, row_cos, row_sin, col_cos, col_sin, weights):
    voxels = field_rows.shape[1]
    phase_angle = field_rows * seg_time
    phase_real = jnp.cos(phase_angle)
    phase_imag = -jnp.sin(phase_angle)
    dir_real = dir_rows[:, :voxels]
    dir_imag = dir_rows[:, voxels:]
    image_real = phase_real * dir_real - phase_imag * dir_imag
    image_imag = phase_real * dir_imag + phase_imag * dir_real
    sens_real = sens_rows[..., :voxels]
    sens_imag = sens_rows[..., voxels:]
    coil_real = sens_real * image_real - sens_imag * image_imag
    coil_imag = sens_real * image_imag + sens_imag * image_real
    grid_real = jnp.einsum('mn,cnv->cmv', row_cos, coil_real, precision=highest) - jnp.einsum('mn,cnv->cmv', row_sin, coil_imag, precision=highest)
    grid_imag = jnp.einsum('mn,cnv->cmv', row_cos, coil_imag, precision=highest) + jnp.einsum('mn,cnv->cmv', row_sin, coil_real, precision=highest)
    kspace_real = jnp.einsum('cmv,vj->cmj', grid_real, col_cos, precision=highest) - jnp.einsum('cmv,vj->cmj', grid_imag, col_sin, precision=highest)
    kspace_imag = jnp.einsum('cmv,vj->cmj', grid_real, col_sin, precision=highest) + jnp.einsum('cmv,vj->cmj', grid_imag, col_cos, precision=highest)
    kspace_real = kspace_real * weights[None]
    kspace_imag = kspace_imag * weights[None]
    back_real = jnp.einsum('cmj,jv->cmv', kspace_real, col_cos, precision=highest) + jnp.einsum('cmj,jv->cmv', kspace_imag, col_sin, precision=highest)
    back_imag = jnp.einsum('cmj,jv->cmv', kspace_imag, col_cos, precision=highest) - jnp.einsum('cmj,jv->cmv', kspace_real, col_sin, precision=highest)
    rows_real = jnp.einsum('mn,cmv->cnv', row_cos, back_real, precision=highest) + jnp.einsum('mn,cmv->cnv', row_sin, back_imag, precision=highest)
    rows_imag = jnp.einsum('mn,cmv->cnv', row_cos, back_imag, precision=highest) - jnp.einsum('mn,cmv->cnv', row_sin, back_real, precision=highest)
    summed_real = lax.optimization_barrier(jnp.sum(sens_real * rows_real + sens_imag * rows_imag, axis=0))
    summed_imag = lax.optimization_barrier(jnp.sum(sens_real * rows_imag - sens_imag * rows_real, axis=0))
    result_real = phase_real * summed_real + phase_imag * summed_imag
    result_imag = phase_real * summed_imag - phase_imag * summed_real
    return jnp.concatenate([result_real, result_imag], axis=1)

def reference(right_side, sensitivity, field_map, seg_map, sample_rows, density, step_alpha, step_beta):
    col_cos, col_sin = column_tables(TV)
    prepared = []
    for segment in range(SEGS):
        listed, valid_slots = tile_list(seg_map, segment, CAP)
        row_cos, row_sin = row_tables(sample_rows[segment], listed, valid_slots, TILES)
        seg_time = jnp.float32((segment + 0.5) / SEGS)
        prepared.append((listed, row_cos, row_sin, seg_time))

    def normal(direction):
        applied = ridge_weight * direction
        for segment in range(SEGS):
            listed, row_cos, row_sin, seg_time = prepared[segment]
            contrib = segment_normal(direction[listed], sensitivity[:, listed], field_map[listed], seg_time, row_cos, row_sin, col_cos, col_sin, density[segment])
            applied = applied.at[listed].add(contrib)
        return applied
    solution_field = jnp.zeros_like(right_side)
    residual = right_side
    direction = right_side
    for step in range(ITERS):
        image = normal(direction)
        solution_field = solution_field + step_alpha[step] * direction
        residual = residual - step_alpha[step] * image
        direction = residual + step_beta[step] * direction
    return (solution_field, residual)
```

```python
import math

import jax
import jax.numpy as jnp
from jax import lax
from jax.sharding import PartitionSpec as P

SEGS = 24
TV = 64
ITERS = 2
CAP = 256
DEVICES = 256


ridge_weight = 0.25
highest = lax.Precision.HIGHEST


def tile_list(seg_map, segment, slots):
    tile_count = seg_map.shape[0]
    is_member = jnp.any(seg_map == segment, axis=1).astype(jnp.int32)
    live_count = jnp.sum(is_member)
    sort_keys = (1 - is_member) * tile_count + jnp.arange(tile_count, dtype=jnp.int32)
    sorted_tiles = jnp.argsort(sort_keys)
    listed = sorted_tiles[:slots]
    valid_slots = (jnp.arange(slots, dtype=jnp.int32) < live_count).astype(jnp.float32)
    return (listed, valid_slots)


def row_tables(rows_here, listed, valid_slots, tile_count):
    product = rows_here[:, None] * listed[None, :] % tile_count
    angles = product.astype(jnp.float32) * jnp.float32(2.0 * math.pi / tile_count)
    slot_scale = valid_slots[None, :] / jnp.float32(math.sqrt(tile_count))
    return (jnp.cos(angles) * slot_scale, -jnp.sin(angles) * slot_scale)


def column_tables(voxels):
    steps_here = jnp.arange(voxels, dtype=jnp.int32)
    product = steps_here[:, None] * steps_here[None, :] % voxels
    angles = product.astype(jnp.float32) * jnp.float32(2.0 * math.pi / voxels)
    norm_factor = jnp.float32(1.0 / math.sqrt(voxels))
    return (jnp.cos(angles) * norm_factor, -jnp.sin(angles) * norm_factor)


def segment_normal(
    dir_rows, sens_rows, field_rows, seg_time, row_cos, row_sin, col_cos, col_sin, weights
):
    voxels = field_rows.shape[1]
    phase_angle = field_rows * seg_time
    phase_real = jnp.cos(phase_angle)
    phase_imag = -jnp.sin(phase_angle)
    dir_real = dir_rows[:, :voxels]
    dir_imag = dir_rows[:, voxels:]
    image_real = phase_real * dir_real - phase_imag * dir_imag
    image_imag = phase_real * dir_imag + phase_imag * dir_real
    sens_real = sens_rows[..., :voxels]
    sens_imag = sens_rows[..., voxels:]
    coil_real = sens_real * image_real - sens_imag * image_imag
    coil_imag = sens_real * image_imag + sens_imag * image_real
    grid_real = jnp.einsum("mn,cnv->cmv", row_cos, coil_real, precision=highest) - jnp.einsum(
        "mn,cnv->cmv", row_sin, coil_imag, precision=highest
    )
    grid_imag = jnp.einsum("mn,cnv->cmv", row_cos, coil_imag, precision=highest) + jnp.einsum(
        "mn,cnv->cmv", row_sin, coil_real, precision=highest
    )
    kspace_real = jnp.einsum("cmv,vj->cmj", grid_real, col_cos, precision=highest) - jnp.einsum(
        "cmv,vj->cmj", grid_imag, col_sin, precision=highest
    )
    kspace_imag = jnp.einsum("cmv,vj->cmj", grid_real, col_sin, precision=highest) + jnp.einsum(
        "cmv,vj->cmj", grid_imag, col_cos, precision=highest
    )
    kspace_real = kspace_real * weights[None]
    kspace_imag = kspace_imag * weights[None]
    back_real = jnp.einsum("cmj,jv->cmv", kspace_real, col_cos, precision=highest) + jnp.einsum(
        "cmj,jv->cmv", kspace_imag, col_sin, precision=highest
    )
    back_imag = jnp.einsum("cmj,jv->cmv", kspace_imag, col_cos, precision=highest) - jnp.einsum(
        "cmj,jv->cmv", kspace_real, col_sin, precision=highest
    )
    rows_real = jnp.einsum("mn,cmv->cnv", row_cos, back_real, precision=highest) + jnp.einsum(
        "mn,cmv->cnv", row_sin, back_imag, precision=highest
    )
    rows_imag = jnp.einsum("mn,cmv->cnv", row_cos, back_imag, precision=highest) - jnp.einsum(
        "mn,cmv->cnv", row_sin, back_real, precision=highest
    )
    summed_real = jnp.sum(sens_real * rows_real + sens_imag * rows_imag, axis=0)
    summed_imag = jnp.sum(sens_real * rows_imag - sens_imag * rows_real, axis=0)
    result_real = phase_real * summed_real + phase_imag * summed_imag
    result_imag = phase_real * summed_imag - phase_imag * summed_real
    return jnp.concatenate([result_real, result_imag], axis=1)


def gather_direction(own_tiles):
    copies = jnp.tile(own_tiles, (DEVICES, 1))
    return lax.all_to_all(copies, ("seg", "coil", "tile"), 0, 0, tiled=True)


def sum_to_owners(partial_value):
    parts = lax.all_to_all(partial_value, ("seg", "coil", "tile"), 0, 0, tiled=True)
    return jnp.sum(parts.reshape(DEVICES, -1, parts.shape[1]), axis=0)


def shards(
    right_side, sensitivity, field_map, seg_map, sample_rows, density, step_alpha, step_beta
):
    seg_local = sample_rows.shape[0]
    tile_count = field_map.shape[0]
    first_segment = lax.axis_index("seg") * seg_local
    col_cos, col_sin = column_tables(TV)
    prepared = []
    for local_seg in range(seg_local):
        segment = first_segment + local_seg
        listed, valid_slots = tile_list(seg_map, segment, CAP)
        row_cos, row_sin = row_tables(sample_rows[local_seg], listed, valid_slots, tile_count)
        seg_time = (segment.astype(jnp.float32) + 0.5) / jnp.float32(SEGS)
        prepared.append(
            (
                listed,
                row_cos,
                row_sin,
                seg_time,
                sensitivity[:, listed],
                field_map[listed],
                density[local_seg],
            )
        )
    direction = right_side
    solution_field = jnp.zeros_like(right_side)
    residual = right_side
    for step in range(ITERS):
        gathered = gather_direction(direction)
        partial_value = jnp.zeros(gathered.shape, jnp.float32)
        for (
            local_listed,
            local_row_cos,
            local_row_sin,
            local_seg_time,
            sens_rows,
            field_rows,
            weights,
        ) in prepared:
            contrib = segment_normal(
                gathered[local_listed],
                sens_rows,
                field_rows,
                local_seg_time,
                local_row_cos,
                local_row_sin,
                col_cos,
                col_sin,
                weights,
            )
            partial_value = partial_value.at[local_listed].add(contrib)
        image = (
            sum_to_owners(partial_value)
            + ridge_weight * direction
        )
        solution_field = solution_field + step_alpha[step] * direction
        residual = residual - step_alpha[step] * image
        direction = residual + step_beta[step] * direction
    return (solution_field, residual)


def solution(mesh):
    placed = (
        P(("seg", "coil", "tile"), None),
        P("coil", None, None),
        P(),
        P(),
        P("seg", "tile"),
        P("seg", "tile", None),
        P(),
        P(),
    )
    return jax.shard_map(
        shards,
        mesh=mesh,
        in_specs=placed,
        out_specs=(P(("seg", "coil", "tile"), None), P(("seg", "coil", "tile"), None)),
        check_vma=False,
    )
```

```python
import math

import jax
import jax.numpy as jnp
import ml_dtypes
import numpy as np
from jax import lax
from jax.experimental import pallas as pl
from jax.experimental.pallas import tpu as pltpu
from jax.sharding import PartitionSpec as P

SEGS = 24
TV = 64
ITERS = 2
DEVICES = 256
TILES = 1024
BLOCKS = 8
SPAN = TILES // BLOCKS
LANES = 2 * TV
AXES = ("seg", "coil", "tile")

ridge_weight = 0.25
half_root = math.sqrt(0.5)


def split_constant(matrix):
    high = matrix.astype(np.float32).astype(ml_dtypes.bfloat16)
    low = (matrix - high.astype(np.float64)).astype(np.float32).astype(ml_dtypes.bfloat16)
    return high, low


def complex_block(real, imag):
    return np.block([[real, -imag], [imag, real]])


def transform_constants():
    steps = np.arange(SPAN)
    row = np.exp(-2j * np.pi * (np.outer(steps, steps) % SPAN) / SPAN)
    row_high, row_low = split_constant(complex_block(row.real, row.imag))
    back_high, back_low = split_constant(complex_block(row.real, -row.imag))
    row_ahead = np.concatenate([row_high, row_low, row_high], axis=1)
    row_back = np.concatenate([back_high, back_low, back_high], axis=1)
    steps = np.arange(TV)
    column = np.exp(-2j * np.pi * (np.outer(steps, steps) % TV) / TV)
    column = np.kron(np.eye(2), column)
    column_high, column_low = split_constant(complex_block(column.real, -column.imag))
    conj_high, conj_low = split_constant(complex_block(column.real, column.imag))
    column_ahead = np.concatenate([column_high, column_high, column_low], axis=0)
    column_back = np.concatenate([conj_high, conj_high, conj_low], axis=0)
    twist = np.exp(-2j * np.pi * np.outer(np.arange(BLOCKS), np.arange(SPAN)) / TILES).reshape(TILES, 1)
    twist = np.stack([twist.real, twist.imag]).astype(np.float32)
    return row_ahead, row_back, column_ahead, column_back, twist


def split(value):
    high = value.astype(jnp.bfloat16)
    low = (value - high.astype(jnp.float32)).astype(jnp.bfloat16)
    return high, low


def four_point(real, imag):
    sum_a, dif_a = (real[0] + real[2], imag[0] + imag[2]), (real[0] - real[2], imag[0] - imag[2])
    sum_b, dif_b = (real[1] + real[3], imag[1] + imag[3]), (real[1] - real[3], imag[1] - imag[3])
    return (
        (sum_a[0] + sum_b[0], sum_a[1] + sum_b[1]),
        (dif_a[0] + dif_b[1], dif_a[1] - dif_b[0]),
        (sum_a[0] - sum_b[0], sum_a[1] - sum_b[1]),
        (dif_a[0] - dif_b[1], dif_a[1] + dif_b[0]),
    )


def eight_point(real, imag):
    even = four_point([real[j] + real[j + 4] for j in range(4)], [imag[j] + imag[j + 4] for j in range(4)])
    dif_real = [real[j] - real[j + 4] for j in range(4)]
    dif_imag = [imag[j] - imag[j + 4] for j in range(4)]
    odd = four_point(
        [
            dif_real[0],
            (dif_real[1] + dif_imag[1]) * half_root,
            dif_imag[2],
            (dif_imag[3] - dif_real[3]) * half_root,
        ],
        [
            dif_imag[0],
            (dif_imag[1] - dif_real[1]) * half_root,
            -dif_real[2],
            (dif_real[3] + dif_imag[3]) * -half_root,
        ],
    )
    return [even[0], odd[0], even[1], odd[1], even[2], odd[2], even[3], odd[3]]


def weights_kernel(rows_ref, density_ref, weights_ref):
    for segment in range(rows_ref.shape[0]):
        rows_here = rows_ref[segment : segment + 1, :]
        density = density_ref[segment]
        high, low = split(jnp.concatenate([density, density], axis=1))
        pieces = jnp.concatenate([high, low], axis=1)
        for block in range(BLOCKS):
            grid_rows = lax.broadcasted_iota(jnp.int32, (SPAN, rows_here.shape[1]), 0) * BLOCKS + block
            chosen = jnp.where(grid_rows == rows_here, 1.0, 0.0).astype(jnp.bfloat16)
            summed = jnp.dot(chosen, pieces, preferred_element_type=jnp.float32)
            weights_ref[segment, pl.ds(block * SPAN, SPAN), :] = (
                summed[:, :LANES] + summed[:, LANES:]
            ) * (1.0 / (TILES * TV))


CHUNK = 16


def normal_kernel(
    dir_ref, maps_ref, weights_ref, twist_ref, row_ref, row_back_ref, col_ref, col_back_ref,
    out_ref, dir_dup, turned, left, left_back, right, back, total,
):
    direction = dir_ref[...]
    rolled = pltpu.roll(direction, TV, 1)
    first_half = lax.broadcasted_iota(jnp.int32, direction.shape, 1) < TV
    dir_dup[0] = jnp.where(first_half, direction, rolled)
    dir_dup[1] = jnp.where(first_half, rolled, direction)
    for segment in range(maps_ref.shape[0]):
        for chunk in range(SPAN // CHUNK):
            at = [pl.ds(block * SPAN + chunk * CHUNK, CHUNK) for block in range(BLOCKS)]
            real, imag = [], []
            for rows in at:
                map_real, map_imag = maps_ref[segment, 0, rows, :], maps_ref[segment, 1, rows, :]
                dir_real, dir_imag = dir_dup[0, rows, :], dir_dup[1, rows, :]
                real.append(map_real * dir_real - map_imag * dir_imag)
                imag.append(map_real * dir_imag + map_imag * dir_real)
            for block, (value_real, value_imag) in enumerate(eight_point(real, imag)):
                if block > 0:
                    twist_real, twist_imag = twist_ref[0, at[block], :], twist_ref[1, at[block], :]
                    value_real, value_imag = (
                        value_real * twist_real - value_imag * twist_imag,
                        value_real * twist_imag + value_imag * twist_real,
                    )
                lanes = pl.ds(block * LANES, LANES)
                for part, value in enumerate((value_real, value_imag)):
                    high, low = split(value)
                    start = part * SPAN + chunk * CHUNK
                    turned[pl.ds(start, CHUNK), lanes] = high
                    turned[pl.ds(2 * SPAN + start, CHUNK), lanes] = high
                    turned[pl.ds(4 * SPAN + start, CHUNK), lanes] = low
        for pair in range(BLOCKS // 2):
            grid = jnp.dot(
                row_ref[...], turned[:, pl.ds(pair * 2 * LANES, 2 * LANES)], preferred_element_type=jnp.float32
            )
            for side in range(2):
                rows = pl.ds((2 * pair + side) * SPAN, SPAN)
                for part in range(2):
                    high, low = split(grid[part * SPAN : (part + 1) * SPAN, side * LANES : (side + 1) * LANES])
                    left[rows, pl.ds(part * LANES, LANES)] = high
                    left[rows, pl.ds((2 + part) * LANES, LANES)] = low
                    left[rows, pl.ds((4 + part) * LANES, LANES)] = high
        for pair in range(BLOCKS // 2):
            rows = pl.ds(pair * 2 * SPAN, 2 * SPAN)
            kspace = jnp.dot(left[rows, :], col_ref[...], preferred_element_type=jnp.float32)
            weights = weights_ref[segment, rows, :]
            high, low = split(kspace * jnp.concatenate([weights, weights], axis=1))
            left_back[rows, pl.ds(0, 2 * LANES)] = high
            left_back[rows, pl.ds(2 * LANES, 2 * LANES)] = low
            left_back[rows, pl.ds(4 * LANES, 2 * LANES)] = high
        for pair in range(BLOCKS // 2):
            rows = pl.ds(pair * 2 * SPAN, 2 * SPAN)
            grid = jnp.dot(left_back[rows, :], col_back_ref[...], preferred_element_type=jnp.float32)
            high, low = split(grid)
            for side in range(2):
                lanes = pl.ds((2 * pair + side) * LANES, LANES)
                for part in range(2):
                    piece = (slice(side * SPAN, (side + 1) * SPAN), slice(part * LANES, (part + 1) * LANES))
                    right[pl.ds(part * SPAN, SPAN), lanes] = high[piece]
                    right[pl.ds((2 + part) * SPAN, SPAN), lanes] = high[piece]
                    right[pl.ds((4 + part) * SPAN, SPAN), lanes] = low[piece]
        for pair in range(BLOCKS // 2):
            lanes = pl.ds(pair * 2 * LANES, 2 * LANES)
            back[:, lanes] = jnp.dot(row_back_ref[...], right[:, lanes], preferred_element_type=jnp.float32)
        for chunk in range(SPAN // CHUNK):
            real, imag = [], []
            for block in range(BLOCKS):
                lanes = pl.ds(block * LANES, LANES)
                value_real = back[pl.ds(chunk * CHUNK, CHUNK), lanes]
                value_imag = back[pl.ds(SPAN + chunk * CHUNK, CHUNK), lanes]
                if block > 0:
                    rows = pl.ds(block * SPAN + chunk * CHUNK, CHUNK)
                    twist_real, twist_imag = twist_ref[0, rows, :], twist_ref[1, rows, :]
                    value_real, value_imag = (
                        value_real * twist_real + value_imag * twist_imag,
                        value_imag * twist_real - value_real * twist_imag,
                    )
                real.append(value_real)
                imag.append(value_imag)
            for block, (value_imag, value_real) in enumerate(eight_point(imag, real)):
                rows = pl.ds(block * SPAN + chunk * CHUNK, CHUNK)
                map_real, map_imag = maps_ref[segment, 0, rows, :], maps_ref[segment, 1, rows, :]
                add_real = map_real * value_real + map_imag * value_imag
                add_imag = map_real * value_imag - map_imag * value_real
                if segment > 0:
                    add_real += total[0, rows, :]
                    add_imag += total[1, rows, :]
                total[0, rows, :] = add_real
                total[1, rows, :] = add_imag
    real, imag = total[0], total[1]
    out_ref[...] = jnp.where(first_half, real + pltpu.roll(real, TV, 1), imag + pltpu.roll(imag, TV, 1))


def in_vmem(count):
    return [pl.BlockSpec(memory_space=pltpu.VMEM)] * count


def sample_weights(sample_rows, density):
    return pl.pallas_call(
        weights_kernel,
        out_shape=jax.ShapeDtypeStruct((sample_rows.shape[0], TILES, LANES), jnp.float32),
        in_specs=in_vmem(2),
        out_specs=pl.BlockSpec(memory_space=pltpu.VMEM),
        compiler_params=pltpu.CompilerParams(vmem_limit_bytes=40 << 20),
        name="sample_weights",
    )(sample_rows, density)


def apply_normal(*operands):
    return pl.pallas_call(
        normal_kernel,
        out_shape=jax.ShapeDtypeStruct((TILES, LANES), jnp.float32),
        in_specs=in_vmem(8),
        out_specs=pl.BlockSpec(memory_space=pltpu.VMEM),
        scratch_shapes=[
            pltpu.VMEM((2, TILES, LANES), jnp.float32),
            pltpu.VMEM((6 * SPAN, BLOCKS * LANES), jnp.bfloat16),
            pltpu.VMEM((TILES, 6 * LANES), jnp.bfloat16),
            pltpu.VMEM((TILES, 6 * LANES), jnp.bfloat16),
            pltpu.VMEM((6 * SPAN, BLOCKS * LANES), jnp.bfloat16),
            pltpu.VMEM((2 * SPAN, BLOCKS * LANES), jnp.float32),
            pltpu.VMEM((2, TILES, LANES), jnp.float32),
        ],
        compiler_params=pltpu.CompilerParams(vmem_limit_bytes=48 << 20),
        name="apply_normal",
    )(*operands)


def coil_maps(sensitivity, field_map, seg_map, first_segment, seg_local):
    sens_real = jnp.concatenate([sensitivity[0, :, :TV], sensitivity[1, :, :TV]], axis=1)
    sens_imag = jnp.concatenate([sensitivity[0, :, TV:], sensitivity[1, :, TV:]], axis=1)
    maps = []
    for local_seg in range(seg_local):
        segment = first_segment + local_seg
        listed = jnp.any(seg_map == segment, axis=1, keepdims=True).astype(jnp.float32)
        angle = field_map * ((segment.astype(jnp.float32) + 0.5) / jnp.float32(SEGS))
        cosine, sine = jnp.cos(angle) * listed, jnp.sin(angle) * listed
        cosine, sine = jnp.concatenate([cosine, cosine], axis=1), jnp.concatenate([sine, sine], axis=1)
        maps.append(jnp.stack([sens_real * cosine + sens_imag * sine, sens_imag * cosine - sens_real * sine]))
    return jnp.stack(maps)


def gather_direction(own_tiles):
    copies = jnp.tile(own_tiles, (DEVICES, 1))
    return lax.all_to_all(copies, AXES, 0, 0, tiled=True)


def sum_to_owners(partial_value):
    parts = lax.all_to_all(partial_value, AXES, 0, 0, tiled=True)
    return jnp.sum(parts.reshape(DEVICES, -1, parts.shape[1]), axis=0)


def shards(
    right_side, sensitivity, field_map, seg_map, sample_rows, density, step_alpha, step_beta
):
    seg_local = sample_rows.shape[0]
    first_segment = lax.axis_index("seg") * seg_local
    row_ahead, row_back, column_ahead, column_back, twist = map(jnp.asarray, transform_constants())
    twist = jnp.broadcast_to(twist, (2, TILES, LANES))
    direction = right_side
    gathered = gather_direction(direction)
    maps = coil_maps(sensitivity, field_map, seg_map, first_segment, seg_local)
    weights = sample_weights(sample_rows, density)
    solution_field = jnp.zeros_like(right_side)
    residual = right_side
    for step in range(ITERS):
        partial_value = apply_normal(
            gathered, maps, weights, twist, row_ahead, row_back, column_ahead, column_back
        )
        image = sum_to_owners(partial_value) + ridge_weight * direction
        solution_field = solution_field + step_alpha[step] * direction
        residual = residual - step_alpha[step] * image
        direction = residual + step_beta[step] * direction
        if step + 1 < ITERS:
            gathered = gather_direction(direction)
    return (solution_field, residual)


def solution(mesh):
    placed = (
        P(AXES, None),
        P("coil", None, None),
        P(),
        P(),
        P("seg", "tile"),
        P("seg", "tile", None),
        P(),
        P(),
    )
    return jax.shard_map(
        shards,
        mesh=mesh,
        in_specs=placed,
        out_specs=(P(AXES, None), P(AXES, None)),
        check_vma=False,
    )
```

```python
import functools
import math

import jax
import jax.numpy as jnp
import ml_dtypes
import numpy as np
from jax import lax
from jax.experimental import pallas as pl
from jax.experimental.pallas import tpu as pltpu
from jax.sharding import PartitionSpec as P

SEGS = 24
TV = 64
DEVICES = 256
TILES = 1024
BLOCKS = 8
SPAN = TILES // BLOCKS
LANES = 2 * TV
SAME_CORE = ("y", "x", "z_lo", "z_hi")

ridge_weight = 0.25
half_root = math.sqrt(0.5)


def split_constant(matrix):
    high = matrix.astype(np.float32).astype(ml_dtypes.bfloat16)
    low = (matrix - high.astype(np.float64)).astype(np.float32).astype(ml_dtypes.bfloat16)
    return high, low


def complex_block(real, imag):
    return np.block([[real, -imag], [imag, real]])


def transform_constants():
    steps = np.arange(SPAN)
    row = np.exp(-2j * np.pi * (np.outer(steps, steps) % SPAN) / SPAN)
    row_high, row_low = split_constant(complex_block(row.real, row.imag))
    back_high, back_low = split_constant(complex_block(row.real, -row.imag))
    row_ahead = np.concatenate([row_high, row_low, row_high], axis=1)
    row_back = np.concatenate([back_high, back_low, back_high], axis=1)
    steps = np.arange(TV)
    column = np.exp(-2j * np.pi * (np.outer(steps, steps) % TV) / TV)
    column = np.kron(np.eye(2), column)
    column_high, column_low = split_constant(complex_block(column.real, -column.imag))
    conj_high, conj_low = split_constant(complex_block(column.real, column.imag))
    column_ahead = np.concatenate([column_high, column_high, column_low], axis=0)
    column_back = np.concatenate([conj_high, conj_high, conj_low], axis=0)
    twist = np.exp(-2j * np.pi * np.outer(np.arange(BLOCKS), np.arange(SPAN)) / TILES).reshape(TILES, 1)
    twist = np.stack([twist.real, twist.imag]).astype(np.float32)
    return row_ahead, row_back, column_ahead, column_back, twist


def split(value):
    high = value.astype(jnp.bfloat16)
    low = (value - high.astype(jnp.float32)).astype(jnp.bfloat16)
    return high, low


def four_point(real, imag):
    sum_a, dif_a = (real[0] + real[2], imag[0] + imag[2]), (real[0] - real[2], imag[0] - imag[2])
    sum_b, dif_b = (real[1] + real[3], imag[1] + imag[3]), (real[1] - real[3], imag[1] - imag[3])
    return (
        (sum_a[0] + sum_b[0], sum_a[1] + sum_b[1]),
        (dif_a[0] + dif_b[1], dif_a[1] - dif_b[0]),
        (sum_a[0] - sum_b[0], sum_a[1] - sum_b[1]),
        (dif_a[0] - dif_b[1], dif_a[1] + dif_b[0]),
    )


def eight_point(real, imag):
    even = four_point([real[j] + real[j + 4] for j in range(4)], [imag[j] + imag[j + 4] for j in range(4)])
    dif_real = [real[j] - real[j + 4] for j in range(4)]
    dif_imag = [imag[j] - imag[j + 4] for j in range(4)]
    odd = four_point(
        [
            dif_real[0],
            (dif_real[1] + dif_imag[1]) * half_root,
            dif_imag[2],
            (dif_imag[3] - dif_real[3]) * half_root,
        ],
        [
            dif_imag[0],
            (dif_imag[1] - dif_real[1]) * half_root,
            -dif_real[2],
            (dif_real[3] + dif_imag[3]) * -half_root,
        ],
    )
    return [even[0], odd[0], even[1], odd[1], even[2], odd[2], even[3], odd[3]]


def cosine_sine(angle):
    turns = jnp.round(angle * (2.0 / math.pi))
    rest = angle - turns * 1.5703125
    rest = rest - turns * 4.837512969970703e-4
    rest = rest - turns * 7.549789948768648e-8
    square = rest * rest
    sine = rest + rest * square * (
        -1.6666654611e-1 + square * (8.3321608736e-3 + square * -1.9515295891e-4)
    )
    cosine = 1.0 - 0.5 * square + square * square * (
        4.166664568298827e-2 + square * (-1.388731625493765e-3 + square * 2.443315711809948e-5)
    )
    quarter = turns.astype(jnp.int32)
    swapped = (quarter & 1) == 1
    flip_cosine = ((quarter + 1) & 2) == 2
    flip_sine = (quarter & 2) == 2
    cosine, sine = jnp.where(swapped, sine, cosine), jnp.where(swapped, cosine, sine)
    return jnp.where(flip_cosine, -cosine, cosine), jnp.where(flip_sine, -sine, sine)


def prepare_kernel(
    first_ref, sens_ref, field_ref, seg_map_ref, rows_ref, density_ref, maps_ref, weights_ref
):
    seg_local = rows_ref.shape[0]
    for block in range(BLOCKS):
        at = pl.ds(block * SPAN, SPAN)
        field = field_ref[at, :]
        field = jnp.concatenate([field, field], axis=1)
        named = seg_map_ref[at, :]
        sens = [sens_ref[coil, at, :] for coil in range(2)]
        sens_real = jnp.concatenate([sens[0][:, :TV], sens[1][:, :TV]], axis=1)
        sens_imag = jnp.concatenate([sens[0][:, TV:], sens[1][:, TV:]], axis=1)
        for local_seg in range(seg_local):
            segment = first_ref[0] + local_seg
            member = jnp.where(named == segment, 1.0, 0.0)
            listed = jnp.where(jnp.sum(member, axis=1, keepdims=True) > 0.0, 1.0, 0.0)
            seg_time = (segment.astype(jnp.float32) + 0.5) / SEGS
            cosine, sine = cosine_sine(field * seg_time)
            cosine, sine = cosine * listed, sine * listed
            maps_ref[local_seg, 0, at, :] = sens_real * cosine + sens_imag * sine
            maps_ref[local_seg, 1, at, :] = sens_imag * cosine - sens_real * sine
    for local_seg in range(seg_local):
        rows_here = rows_ref[local_seg : local_seg + 1, :]
        density = density_ref[local_seg]
        high, low = split(jnp.concatenate([density, density], axis=1))
        pieces = jnp.concatenate([high, low], axis=1)
        for block in range(BLOCKS):
            grid_rows = lax.broadcasted_iota(jnp.int32, (SPAN, rows_here.shape[1]), 0) * BLOCKS + block
            chosen = jnp.where(grid_rows == rows_here, 1.0, 0.0).astype(jnp.bfloat16)
            summed = jnp.dot(chosen, pieces, preferred_element_type=jnp.float32)
            weights_ref[local_seg, pl.ds(block * SPAN, SPAN), :] = (
                summed[:, :LANES] + summed[:, LANES:]
            ) * (1.0 / (TILES * TV))


CHUNK = 16


def normal_kernel(further, core_ref, *refs):
    if further:
        alpha_ref, beta_ref, mine_ref, other_ref, mine_sum_ref, other_sum_ref = refs[:6]
        refs = refs[6:]
    else:
        mine_ref, other_ref = refs[:2]
        refs = refs[2:]
    maps_ref, weights_ref, twist_ref, row_ref, row_back_ref, col_ref, col_back_ref = refs[:7]
    keep_ref, send_ref, dir_dup, turned, left, left_back, right, back, total = refs[7:]
    core = core_ref[0]
    first_half = lax.broadcasted_iota(jnp.int32, (SPAN, LANES), 1) < TV
    for pair in range(BLOCKS // 2):
        for whose in range(2):
            from_rows = pl.ds(pair * SPAN, SPAN)
            to_rows = pl.ds((2 * pair + (core if whose == 0 else 1 - core)) * SPAN, SPAN)
            direction = (mine_ref, other_ref)[whose][from_rows, :]
            if further:
                image = (mine_sum_ref, other_sum_ref)[whose][from_rows, :] + ridge_weight * direction
                direction = direction - alpha_ref[0] * image + beta_ref[0] * direction
            rolled = pltpu.roll(direction, TV, 1)
            dir_dup[0, to_rows, :] = jnp.where(first_half, direction, rolled)
            dir_dup[1, to_rows, :] = jnp.where(first_half, rolled, direction)
    for segment in range(maps_ref.shape[0]):
        for chunk in range(SPAN // CHUNK):
            at = [pl.ds(block * SPAN + chunk * CHUNK, CHUNK) for block in range(BLOCKS)]
            real, imag = [], []
            for rows in at:
                map_real, map_imag = maps_ref[segment, 0, rows, :], maps_ref[segment, 1, rows, :]
                dir_real, dir_imag = dir_dup[0, rows, :], dir_dup[1, rows, :]
                real.append(map_real * dir_real - map_imag * dir_imag)
                imag.append(map_real * dir_imag + map_imag * dir_real)
            for block, (value_real, value_imag) in enumerate(eight_point(real, imag)):
                if block > 0:
                    twist_real, twist_imag = twist_ref[0, at[block], :], twist_ref[1, at[block], :]
                    value_real, value_imag = (
                        value_real * twist_real - value_imag * twist_imag,
                        value_real * twist_imag + value_imag * twist_real,
                    )
                lanes = pl.ds(block * LANES, LANES)
                for part, value in enumerate((value_real, value_imag)):
                    high, low = split(value)
                    start = part * SPAN + chunk * CHUNK
                    turned[pl.ds(start, CHUNK), lanes] = high
                    turned[pl.ds(2 * SPAN + start, CHUNK), lanes] = high
                    turned[pl.ds(4 * SPAN + start, CHUNK), lanes] = low
        for pair in range(BLOCKS // 2):
            grid = jnp.dot(
                row_ref[...], turned[:, pl.ds(pair * 2 * LANES, 2 * LANES)], preferred_element_type=jnp.float32
            )
            for side in range(2):
                rows = pl.ds((2 * pair + side) * SPAN, SPAN)
                for part in range(2):
                    high, low = split(grid[part * SPAN : (part + 1) * SPAN, side * LANES : (side + 1) * LANES])
                    left[rows, pl.ds(part * LANES, LANES)] = high
                    left[rows, pl.ds((2 + part) * LANES, LANES)] = low
                    left[rows, pl.ds((4 + part) * LANES, LANES)] = high
        for pair in range(BLOCKS // 2):
            rows = pl.ds(pair * 2 * SPAN, 2 * SPAN)
            kspace = jnp.dot(left[rows, :], col_ref[...], preferred_element_type=jnp.float32)
            weights = weights_ref[segment, rows, :]
            high, low = split(kspace * jnp.concatenate([weights, weights], axis=1))
            left_back[rows, pl.ds(0, 2 * LANES)] = high
            left_back[rows, pl.ds(2 * LANES, 2 * LANES)] = low
            left_back[rows, pl.ds(4 * LANES, 2 * LANES)] = high
        for pair in range(BLOCKS // 2):
            rows = pl.ds(pair * 2 * SPAN, 2 * SPAN)
            grid = jnp.dot(left_back[rows, :], col_back_ref[...], preferred_element_type=jnp.float32)
            high, low = split(grid)
            for side in range(2):
                lanes = pl.ds((2 * pair + side) * LANES, LANES)
                for part in range(2):
                    piece = (slice(side * SPAN, (side + 1) * SPAN), slice(part * LANES, (part + 1) * LANES))
                    right[pl.ds(part * SPAN, SPAN), lanes] = high[piece]
                    right[pl.ds((2 + part) * SPAN, SPAN), lanes] = high[piece]
                    right[pl.ds((4 + part) * SPAN, SPAN), lanes] = low[piece]
        for pair in range(BLOCKS // 2):
            lanes = pl.ds(pair * 2 * LANES, 2 * LANES)
            back[:, lanes] = jnp.dot(row_back_ref[...], right[:, lanes], preferred_element_type=jnp.float32)
        for chunk in range(SPAN // CHUNK):
            real, imag = [], []
            for block in range(BLOCKS):
                lanes = pl.ds(block * LANES, LANES)
                value_real = back[pl.ds(chunk * CHUNK, CHUNK), lanes]
                value_imag = back[pl.ds(SPAN + chunk * CHUNK, CHUNK), lanes]
                if block > 0:
                    rows = pl.ds(block * SPAN + chunk * CHUNK, CHUNK)
                    twist_real, twist_imag = twist_ref[0, rows, :], twist_ref[1, rows, :]
                    value_real, value_imag = (
                        value_real * twist_real + value_imag * twist_imag,
                        value_imag * twist_real - value_real * twist_imag,
                    )
                real.append(value_real)
                imag.append(value_imag)
            for block, (value_imag, value_real) in enumerate(eight_point(imag, real)):
                rows = pl.ds(block * SPAN + chunk * CHUNK, CHUNK)
                map_real, map_imag = maps_ref[segment, 0, rows, :], maps_ref[segment, 1, rows, :]
                add_real = map_real * value_real + map_imag * value_imag
                add_imag = map_real * value_imag - map_imag * value_real
                if segment > 0:
                    add_real += total[0, rows, :]
                    add_imag += total[1, rows, :]
                total[0, rows, :] = add_real
                total[1, rows, :] = add_imag
    for pair in range(BLOCKS // 2):
        for whose, out_ref in enumerate((keep_ref, send_ref)):
            rows = pl.ds((2 * pair + (core if whose == 0 else 1 - core)) * SPAN, SPAN)
            real, imag = total[0, rows, :], total[1, rows, :]
            out_ref[pl.ds(pair * SPAN, SPAN), :] = jnp.where(
                first_half, real + pltpu.roll(real, TV, 1), imag + pltpu.roll(imag, TV, 1)
            )


def specs(scalars, arrays):
    return [pl.BlockSpec(memory_space=pltpu.SMEM)] * scalars + [pl.BlockSpec(memory_space=pltpu.VMEM)] * arrays


def prepare(first_segment, sensitivity, field_map, seg_map, sample_rows, density):
    seg_local = sample_rows.shape[0]
    return pl.pallas_call(
        prepare_kernel,
        out_shape=(
            jax.ShapeDtypeStruct((seg_local, 2, TILES, LANES), jnp.float32),
            jax.ShapeDtypeStruct((seg_local, TILES, LANES), jnp.float32),
        ),
        in_specs=specs(1, 5),
        out_specs=tuple(specs(0, 2)),
        compiler_params=pltpu.CompilerParams(vmem_limit_bytes=16 << 20),
        name="maps_and_weights",
    )(first_segment, sensitivity, field_map, seg_map, sample_rows, density)


def apply_normal(core, steps, directions, tables):
    half = jax.ShapeDtypeStruct((TILES // 2, LANES), jnp.float32)
    return pl.pallas_call(
        functools.partial(normal_kernel, len(steps) > 0),
        out_shape=(half, half),
        in_specs=specs(1 + len(steps), len(directions) + len(tables)),
        out_specs=tuple(specs(0, 2)),
        scratch_shapes=[
            pltpu.VMEM((2, TILES, LANES), jnp.float32),
            pltpu.VMEM((6 * SPAN, BLOCKS * LANES), jnp.bfloat16),
            pltpu.VMEM((TILES, 6 * LANES), jnp.bfloat16),
            pltpu.VMEM((TILES, 6 * LANES), jnp.bfloat16),
            pltpu.VMEM((6 * SPAN, BLOCKS * LANES), jnp.bfloat16),
            pltpu.VMEM((2 * SPAN, BLOCKS * LANES), jnp.float32),
            pltpu.VMEM((2, TILES, LANES), jnp.float32),
        ],
        compiler_params=pltpu.CompilerParams(vmem_limit_bytes=20 << 20),
        name="apply_normal",
    )(core, *steps, *directions, *tables)


def swap_cores(value):
    return lax.ppermute(value, "core", [(0, 1), (1, 0)])


def exchange(value, axes):
    return lax.all_to_all(value, axes, 0, 0, tiled=True)


def summed(parts, count):
    return jnp.sum(parts.reshape(count, -1, LANES), axis=0)


def gather_direction(own_tiles):
    mine = exchange(jnp.tile(own_tiles, (DEVICES // 2, 1)), SAME_CORE)
    return mine, swap_cores(mine)


def sum_to_owners(keep, send):
    return summed(exchange(keep + swap_cores(send), SAME_CORE), DEVICES // 2)


def sum_for_all(keep, send):
    share = summed(exchange(keep + swap_cores(send), ("y", "x")), 16)
    share = summed(exchange(jnp.tile(share, (8, 1)), ("z_lo", "z_hi")), 8)
    mine = exchange(jnp.tile(share, (16, 1)), ("y", "x"))
    return mine, swap_cores(mine)


def shards(
    right_side, sensitivity, field_map, seg_map, sample_rows, density, step_alpha, step_beta
):
    seg_local = sample_rows.shape[0]
    first_segment = lax.axis_index(("y", "core")) * seg_local
    core = lax.axis_index("core").reshape(1)
    row_ahead, row_back, column_ahead, column_back, twist = map(jnp.asarray, transform_constants())
    twist = jnp.broadcast_to(twist, (2, TILES, LANES))
    gathered = gather_direction(right_side)
    maps, weights = prepare(
        first_segment.reshape(1), sensitivity, field_map, seg_map, sample_rows, density
    )
    tables = (maps, weights, twist, row_ahead, row_back, column_ahead, column_back)
    sums = sum_for_all(*apply_normal(core, (), gathered, tables))
    own_tiles = right_side.shape[0]
    own_start = lax.axis_index(SAME_CORE) * own_tiles
    own_sum = lax.dynamic_slice_in_dim(sums[0], own_start, own_tiles, 0)
    solution_field = step_alpha[0] * right_side
    residual = right_side - step_alpha[0] * (own_sum + ridge_weight * right_side)
    direction = residual + step_beta[0] * right_side
    last_sum = sum_to_owners(
        *apply_normal(core, (step_alpha, step_beta), (*gathered, *sums), tables)
    )
    solution_field = solution_field + step_alpha[1] * direction
    residual = residual - step_alpha[1] * (last_sum + ridge_weight * direction)
    return (solution_field, residual)


def solution(mesh):
    axes = ("y", "core", "x", "z_lo", "z_hi")
    fine_mesh = jax.sharding.Mesh(mesh.devices.reshape(4, 2, 4, 4, 2), axes)
    seg, coil, tile = ("y", "core"), ("x", "z_lo"), "z_hi"
    placed = (
        P(axes, None),
        P(coil, None, None),
        P(),
        P(),
        P(seg, tile),
        P(seg, tile, None),
        P(),
        P(),
    )
    return jax.shard_map(
        shards,
        mesh=fine_mesh,
        in_specs=placed,
        out_specs=(P(axes, None), P(axes, None)),
        check_vma=False,
    )
```

```python
import functools
import math

import jax
import jax.numpy as jnp
import ml_dtypes
import numpy as np
from jax import lax
from jax.experimental import pallas as pl
from jax.experimental.pallas import tpu as pltpu
from jax.sharding import PartitionSpec as P

SEGS = 24
TV = 64
DEVICES = 256
TILES = 1024
BLOCKS = 8
SPAN = TILES // BLOCKS
LANES = 2 * TV
SAME_CORE = ("y", "x", "z_lo", "z_hi")

ridge_weight = 0.25
half_root = math.sqrt(0.5)


def split_constant(matrix):
    high = matrix.astype(np.float32).astype(ml_dtypes.bfloat16)
    low = (matrix - high.astype(np.float64)).astype(np.float32).astype(ml_dtypes.bfloat16)
    return high, low


def complex_block(real, imag):
    return np.block([[real, -imag], [imag, real]])


def transform_constants():
    steps = np.arange(SPAN)
    row = np.exp(-2j * np.pi * (np.outer(steps, steps) % SPAN) / SPAN)
    row_high, row_low = split_constant(complex_block(row.real, row.imag))
    back_high, back_low = split_constant(complex_block(row.real, -row.imag))
    row_ahead = np.concatenate([row_high, row_low, row_high], axis=1)
    row_back = np.concatenate([back_high, back_low, back_high], axis=1)
    steps = np.arange(TV)
    column = np.exp(-2j * np.pi * (np.outer(steps, steps) % TV) / TV)
    column = np.kron(np.eye(2), column)
    column_high, column_low = split_constant(complex_block(column.real, -column.imag))
    conj_high, conj_low = split_constant(complex_block(column.real, column.imag))
    column_ahead = np.concatenate([column_high, column_high, column_low], axis=0)
    column_back = np.concatenate([conj_high, conj_high, conj_low], axis=0)
    twist = np.exp(-2j * np.pi * np.outer(np.arange(BLOCKS), np.arange(SPAN)) / TILES)
    twist = np.stack([twist.real, twist.imag]).astype(np.float32)
    return row_ahead, row_back, column_ahead, column_back, twist


def split(value):
    high = value.astype(jnp.bfloat16)
    low = (value - high.astype(jnp.float32)).astype(jnp.bfloat16)
    return high, low


def four_point(real, imag):
    sum_a, dif_a = (real[0] + real[2], imag[0] + imag[2]), (real[0] - real[2], imag[0] - imag[2])
    sum_b, dif_b = (real[1] + real[3], imag[1] + imag[3]), (real[1] - real[3], imag[1] - imag[3])
    return (
        (sum_a[0] + sum_b[0], sum_a[1] + sum_b[1]),
        (dif_a[0] + dif_b[1], dif_a[1] - dif_b[0]),
        (sum_a[0] - sum_b[0], sum_a[1] - sum_b[1]),
        (dif_a[0] - dif_b[1], dif_a[1] + dif_b[0]),
    )


def eight_point(real, imag):
    even = four_point([real[j] + real[j + 4] for j in range(4)], [imag[j] + imag[j + 4] for j in range(4)])
    dif_real = [real[j] - real[j + 4] for j in range(4)]
    dif_imag = [imag[j] - imag[j + 4] for j in range(4)]
    odd = four_point(
        [
            dif_real[0],
            (dif_real[1] + dif_imag[1]) * half_root,
            dif_imag[2],
            (dif_imag[3] - dif_real[3]) * half_root,
        ],
        [
            dif_imag[0],
            (dif_imag[1] - dif_real[1]) * half_root,
            -dif_real[2],
            (dif_real[3] + dif_imag[3]) * -half_root,
        ],
    )
    return [even[0], odd[0], even[1], odd[1], even[2], odd[2], even[3], odd[3]]


def cosine_sine(angle):
    turns = jnp.round(angle * (2.0 / math.pi))
    rest = angle - turns * 1.5703125
    rest = rest - turns * 4.837512969970703e-4
    rest = rest - turns * 7.549789948768648e-8
    square = rest * rest
    sine = rest + rest * square * (
        -1.6666654611e-1 + square * (8.3321608736e-3 + square * -1.9515295891e-4)
    )
    cosine = 1.0 - 0.5 * square + square * square * (
        4.166664568298827e-2 + square * (-1.388731625493765e-3 + square * 2.443315711809948e-5)
    )
    quarter = turns.astype(jnp.int32)
    swapped = (quarter & 1) == 1
    flip_cosine = ((quarter + 1) & 2) == 2
    flip_sine = (quarter & 2) == 2
    cosine, sine = jnp.where(swapped, sine, cosine), jnp.where(swapped, cosine, sine)
    return jnp.where(flip_cosine, -cosine, cosine), jnp.where(flip_sine, -sine, sine)


def prepare_kernel(
    first_ref, sens_ref, field_ref, seg_map_ref, rows_ref, density_ref, turns_ref,
    maps_ref, weights_ref, twist_ref,
):
    seg_local = rows_ref.shape[0]
    for block in range(BLOCKS):
        at = pl.ds(block * SPAN, SPAN)
        for part in range(2):
            twist_ref[part, at, :] = jnp.broadcast_to(turns_ref[part, block : block + 1, :], (SPAN, LANES)).T
        field = field_ref[:, at]
        field = jnp.concatenate([field, field], axis=0).T
        named = seg_map_ref[:, at]
        listed = []
        for local_seg in range(seg_local):
            member = jnp.where(named == first_ref[0] + local_seg, 1.0, 0.0)
            listed.append(jnp.where(jnp.sum(member, axis=0, keepdims=True) > 0.0, 1.0, 0.0))
        listed.append(jnp.zeros((8 - seg_local, SPAN), jnp.float32))
        listed = jnp.concatenate(listed, axis=0).T
        sens = [sens_ref[coil, at, :] for coil in range(2)]
        sens_real = jnp.concatenate([sens[0][:, :TV], sens[1][:, :TV]], axis=1)
        sens_imag = jnp.concatenate([sens[0][:, TV:], sens[1][:, TV:]], axis=1)
        for local_seg in range(seg_local):
            segment = first_ref[0] + local_seg
            seg_time = (segment.astype(jnp.float32) + 0.5) / SEGS
            cosine, sine = cosine_sine(field * seg_time)
            live = listed[:, local_seg : local_seg + 1]
            cosine, sine = cosine * live, sine * live
            maps_ref[local_seg, 0, at, :] = sens_real * cosine + sens_imag * sine
            maps_ref[local_seg, 1, at, :] = sens_imag * cosine - sens_real * sine
    for local_seg in range(seg_local):
        rows_here = rows_ref[local_seg : local_seg + 1, :]
        high, low = split(density_ref[local_seg])
        pieces = jnp.concatenate([high, high, low, low], axis=0)
        for block in range(BLOCKS):
            grid_rows = lax.broadcasted_iota(jnp.int32, (SPAN, rows_here.shape[1]), 0) * BLOCKS + block
            chosen = jnp.where(grid_rows == rows_here, 1.0, 0.0).astype(jnp.bfloat16)
            summed = lax.dot_general(
                chosen, pieces, (((1,), (1,)), ((), ())), preferred_element_type=jnp.float32
            )
            weights_ref[local_seg, pl.ds(block * SPAN, SPAN), :] = (
                summed[:, :LANES] + summed[:, LANES:]
            ) * (1.0 / (TILES * TV))


def share_kernel(parts_ref, out_ref):
    value = jnp.sum(parts_ref[...], axis=0)
    for copy in range(out_ref.shape[0]):
        out_ref[copy] = value


def update_kernel(alpha_ref, beta_ref, parts_ref, right_ref, own_ref, solution_ref, residual_ref):
    eight = jnp.sum(parts_ref[...], axis=0)
    own_rows = right_ref.shape[0]
    last_sum = eight[:own_rows] + eight[own_rows:]
    right = right_ref[...]
    residual = right - alpha_ref[0] * (own_ref[...] + ridge_weight * right)
    direction = residual + beta_ref[0] * right
    solution_ref[...] = alpha_ref[0] * right + alpha_ref[1] * direction
    residual_ref[...] = residual - alpha_ref[1] * (last_sum + ridge_weight * direction)


CHUNK = 16


def normal_kernel(further, core_ref, *refs):
    if further:
        alpha_ref, beta_ref, mine_ref, other_ref, mine_sum_ref, other_sum_ref = refs[:6]
        refs = refs[6:]
    else:
        mine_ref, other_ref = refs[:2]
        refs = refs[2:]
    sources = refs[:7]
    keep_ref, send_ref, dir_dup, turned, left, left_back, right, back, total = refs[7:16]
    held, arrived = refs[16:23], refs[23]
    maps_ref, weights_ref, twist_ref, row_ref, row_back_ref, col_ref, col_back_ref = held
    copies = {}

    def fetch(table, part=None):
        source, target = sources[table], held[table]
        if part is not None:
            source, target = source.at[part], target.at[part]
        copy = pltpu.make_async_copy(source, target, arrived.at[len(copies)])
        copy.start()
        copies[table, part] = copy

    fetch(0, 0)
    fetch(2)
    fetch(3)
    fetch(5)
    fetch(1, 0)
    fetch(6)
    fetch(4)
    for segment in range(1, maps_ref.shape[0]):
        fetch(0, segment)
        fetch(1, segment)
    core = core_ref[0]
    first_half = lax.broadcasted_iota(jnp.int32, (SPAN, LANES), 1) < TV
    for pair in range(BLOCKS // 2):
        for whose in range(2):
            from_rows = pl.ds(pair * SPAN, SPAN)
            to_rows = pl.ds((2 * pair + (core if whose == 0 else 1 - core)) * SPAN, SPAN)
            direction = (mine_ref, other_ref)[whose][from_rows, :]
            if further:
                image = (mine_sum_ref, other_sum_ref)[whose][from_rows, :] + ridge_weight * direction
                direction = direction - alpha_ref[0] * image + beta_ref[0] * direction
            rolled = pltpu.roll(direction, TV, 1)
            dir_dup[0, to_rows, :] = jnp.where(first_half, direction, rolled)
            dir_dup[1, to_rows, :] = jnp.where(first_half, rolled, direction)
    for segment in range(maps_ref.shape[0]):
        copies[0, segment].wait()
        if segment == 0:
            copies[2, None].wait()
        for chunk in range(SPAN // CHUNK):
            at = [pl.ds(block * SPAN + chunk * CHUNK, CHUNK) for block in range(BLOCKS)]
            real, imag = [], []
            for rows in at:
                map_real, map_imag = maps_ref[segment, 0, rows, :], maps_ref[segment, 1, rows, :]
                dir_real, dir_imag = dir_dup[0, rows, :], dir_dup[1, rows, :]
                real.append(map_real * dir_real - map_imag * dir_imag)
                imag.append(map_real * dir_imag + map_imag * dir_real)
            for block, (value_real, value_imag) in enumerate(eight_point(real, imag)):
                if block > 0:
                    twist_real, twist_imag = twist_ref[0, at[block], :], twist_ref[1, at[block], :]
                    value_real, value_imag = (
                        value_real * twist_real - value_imag * twist_imag,
                        value_real * twist_imag + value_imag * twist_real,
                    )
                lanes = pl.ds(block * LANES, LANES)
                for part, value in enumerate((value_real, value_imag)):
                    high, low = split(value)
                    start = part * SPAN + chunk * CHUNK
                    turned[pl.ds(start, CHUNK), lanes] = high
                    turned[pl.ds(2 * SPAN + start, CHUNK), lanes] = high
                    turned[pl.ds(4 * SPAN + start, CHUNK), lanes] = low
        if segment == 0:
            copies[3, None].wait()
        for pair in range(BLOCKS // 2):
            grid = jnp.dot(
                row_ref[...], turned[:, pl.ds(pair * 2 * LANES, 2 * LANES)], preferred_element_type=jnp.float32
            )
            for side in range(2):
                rows = pl.ds((2 * pair + side) * SPAN, SPAN)
                for part in range(2):
                    high, low = split(grid[part * SPAN : (part + 1) * SPAN, side * LANES : (side + 1) * LANES])
                    left[rows, pl.ds(part * LANES, LANES)] = high
                    left[rows, pl.ds((2 + part) * LANES, LANES)] = low
                    left[rows, pl.ds((4 + part) * LANES, LANES)] = high
        copies[1, segment].wait()
        if segment == 0:
            copies[5, None].wait()
            copies[6, None].wait()
            copies[4, None].wait()
        for pair in range(BLOCKS // 2):
            rows = pl.ds(pair * 2 * SPAN, 2 * SPAN)
            kspace = jnp.dot(left[rows, :], col_ref[...], preferred_element_type=jnp.float32)
            weights = weights_ref[segment, rows, :]
            high, low = split(kspace * jnp.concatenate([weights, weights], axis=1))
            left_back[rows, pl.ds(0, 2 * LANES)] = high
            left_back[rows, pl.ds(2 * LANES, 2 * LANES)] = low
            left_back[rows, pl.ds(4 * LANES, 2 * LANES)] = high
        for pair in range(BLOCKS // 2):
            rows = pl.ds(pair * 2 * SPAN, 2 * SPAN)
            grid = jnp.dot(left_back[rows, :], col_back_ref[...], preferred_element_type=jnp.float32)
            high, low = split(grid)
            for side in range(2):
                lanes = pl.ds((2 * pair + side) * LANES, LANES)
                for part in range(2):
                    piece = (slice(side * SPAN, (side + 1) * SPAN), slice(part * LANES, (part + 1) * LANES))
                    right[pl.ds(part * SPAN, SPAN), lanes] = high[piece]
                    right[pl.ds((2 + part) * SPAN, SPAN), lanes] = high[piece]
                    right[pl.ds((4 + part) * SPAN, SPAN), lanes] = low[piece]
        for pair in range(BLOCKS // 2):
            lanes = pl.ds(pair * 2 * LANES, 2 * LANES)
            back[:, lanes] = jnp.dot(row_back_ref[...], right[:, lanes], preferred_element_type=jnp.float32)
        for chunk in range(SPAN // CHUNK):
            real, imag = [], []
            for block in range(BLOCKS):
                lanes = pl.ds(block * LANES, LANES)
                value_real = back[pl.ds(chunk * CHUNK, CHUNK), lanes]
                value_imag = back[pl.ds(SPAN + chunk * CHUNK, CHUNK), lanes]
                if block > 0:
                    rows = pl.ds(block * SPAN + chunk * CHUNK, CHUNK)
                    twist_real, twist_imag = twist_ref[0, rows, :], twist_ref[1, rows, :]
                    value_real, value_imag = (
                        value_real * twist_real + value_imag * twist_imag,
                        value_imag * twist_real - value_real * twist_imag,
                    )
                real.append(value_real)
                imag.append(value_imag)
            for block, (value_imag, value_real) in enumerate(eight_point(imag, real)):
                rows = pl.ds(block * SPAN + chunk * CHUNK, CHUNK)
                map_real, map_imag = maps_ref[segment, 0, rows, :], maps_ref[segment, 1, rows, :]
                add_real = map_real * value_real + map_imag * value_imag
                add_imag = map_real * value_imag - map_imag * value_real
                if segment > 0:
                    add_real += total[0, rows, :]
                    add_imag += total[1, rows, :]
                total[0, rows, :] = add_real
                total[1, rows, :] = add_imag
    for pair in range(BLOCKS // 2):
        for whose, out_ref in enumerate((keep_ref, send_ref)):
            rows = pl.ds((2 * pair + (core if whose == 0 else 1 - core)) * SPAN, SPAN)
            real, imag = total[0, rows, :], total[1, rows, :]
            out_ref[pl.ds(pair * SPAN, SPAN), :] = jnp.where(
                first_half, real + pltpu.roll(real, TV, 1), imag + pltpu.roll(imag, TV, 1)
            )


def specs(scalars, arrays, in_place=0):
    return (
        [pl.BlockSpec(memory_space=pltpu.SMEM)] * scalars
        + [pl.BlockSpec(memory_space=pltpu.VMEM)] * arrays
        + [pl.BlockSpec(memory_space=pltpu.HBM)] * in_place
    )


def prepare(first_segment, sensitivity, field_map, seg_map, sample_rows, density, turns):
    seg_local, samples = sample_rows.shape
    return pl.pallas_call(
        prepare_kernel,
        out_shape=(
            jax.ShapeDtypeStruct((seg_local, 2, TILES, LANES), jnp.float32),
            jax.ShapeDtypeStruct((seg_local, TILES, LANES), jnp.float32),
            jax.ShapeDtypeStruct((2, TILES, LANES), jnp.float32),
        ),
        in_specs=specs(1, 6),
        out_specs=tuple(specs(0, 3)),
        compiler_params=pltpu.CompilerParams(vmem_limit_bytes=16 << 20),
        cost_estimate=pl.CostEstimate(
            flops=2 * seg_local * TILES * samples * 2 * LANES,
            transcendentals=2 * seg_local * TILES * LANES,
            bytes_accessed=4 * seg_local * (3 * TILES * LANES + samples * TV) + 8 * TILES * LANES,
        ),
        name="maps_and_weights",
    )(first_segment, sensitivity, field_map.T, seg_map.T, sample_rows, jnp.swapaxes(density, 1, 2), turns)


def apply_normal(core, steps, directions, tables):
    half = jax.ShapeDtypeStruct((TILES // 2, LANES), jnp.float32)
    segments = tables[0].shape[0]
    return pl.pallas_call(
        functools.partial(normal_kernel, len(steps) > 0),
        out_shape=(half, half),
        in_specs=specs(1 + len(steps), len(directions), len(tables)),
        out_specs=tuple(specs(0, 2)),
        scratch_shapes=[
            pltpu.VMEM((2, TILES, LANES), jnp.float32),
            pltpu.VMEM((6 * SPAN, BLOCKS * LANES), jnp.bfloat16),
            pltpu.VMEM((TILES, 6 * LANES), jnp.bfloat16),
            pltpu.VMEM((TILES, 6 * LANES), jnp.bfloat16),
            pltpu.VMEM((6 * SPAN, BLOCKS * LANES), jnp.bfloat16),
            pltpu.VMEM((2 * SPAN, BLOCKS * LANES), jnp.float32),
            pltpu.VMEM((2, TILES, LANES), jnp.float32),
        ]
        + [pltpu.VMEM(table.shape, table.dtype) for table in tables]
        + [pltpu.SemaphoreType.DMA((5 + 2 * segments,))],
        compiler_params=pltpu.CompilerParams(vmem_limit_bytes=60 << 20),
        cost_estimate=pl.CostEstimate(
            flops=12 * segments * TILES * 6 * LANES * 4 * LANES,
            transcendentals=0,
            bytes_accessed=4 * segments * 4 * TILES * LANES,
        ),
        name="apply_normal",
    )(core, *steps, *directions, *tables)


def swap_cores(value):
    return lax.ppermute(value, "core", [(0, 1), (1, 0)])


def exchange(value, axes):
    return lax.all_to_all(value, axes, 0, 0, tiled=True)


def share(parts, count, copies):
    rows = parts.shape[0] // count
    shared = pl.pallas_call(
        share_kernel,
        out_shape=jax.ShapeDtypeStruct((copies, rows, LANES), jnp.float32),
        in_specs=specs(0, 1),
        out_specs=specs(0, 1)[0],
        name="sum_and_copy",
    )(parts.reshape(count, rows, LANES))
    return shared.reshape(copies * rows, LANES)


def gather_direction(own_tiles):
    return exchange(jnp.tile(own_tiles, (DEVICES // 2, 1)), SAME_CORE)


def sum_to_owners(keep, send):
    return exchange(keep + swap_cores(send), SAME_CORE)


def sum_for_all(keep, send):
    copies = share(exchange(keep + swap_cores(send), ("y", "x")), 16, 8)
    copies = share(exchange(copies, ("z_lo", "z_hi")), 8, 16)
    mine = exchange(copies, ("y", "x"))
    return mine, swap_cores(mine)


def update(step_alpha, step_beta, parts, right_side, own_sum):
    own = jax.ShapeDtypeStruct(right_side.shape, jnp.float32)
    return pl.pallas_call(
        update_kernel,
        out_shape=(own, own),
        in_specs=specs(2, 3),
        out_specs=tuple(specs(0, 2)),
        name="last_update",
    )(step_alpha, step_beta, parts.reshape(-1, 2 * right_side.shape[0], LANES), right_side, own_sum)


def shards(
    right_side, sensitivity, field_map, seg_map, sample_rows, density, step_alpha, step_beta
):
    seg_local = sample_rows.shape[0]
    first_segment = lax.axis_index(("y", "core")) * seg_local
    core = lax.axis_index("core").reshape(1)
    row_ahead, row_back, column_ahead, column_back, turns = map(jnp.asarray, transform_constants())
    gathered = gather_direction(right_side)
    maps, weights, twist = prepare(
        first_segment.reshape(1), sensitivity, field_map, seg_map, sample_rows, density, turns
    )
    gathered, maps, weights, twist = lax.optimization_barrier((gathered, maps, weights, twist))
    gathered = (gathered, swap_cores(gathered))
    tables = (maps, weights, twist, row_ahead, row_back, column_ahead, column_back)
    sums = sum_for_all(*apply_normal(core, (), gathered, tables))
    own_tiles = right_side.shape[0]
    own_start = lax.axis_index(SAME_CORE) * own_tiles
    own_sum = lax.dynamic_slice_in_dim(sums[0], own_start, own_tiles, 0)
    parts = sum_to_owners(
        *apply_normal(core, (step_alpha, step_beta), (*gathered, *sums), tables)
    )
    return update(step_alpha, step_beta, parts, right_side, own_sum)


def solution(mesh):
    axes = ("y", "core", "x", "z_lo", "z_hi")
    fine_mesh = jax.sharding.Mesh(mesh.devices.reshape(4, 2, 4, 4, 2), axes)
    seg, coil, tile = ("y", "core"), ("x", "z_lo"), "z_hi"
    placed = (
        P(axes, None),
        P(coil, None, None),
        P(),
        P(),
        P(seg, tile),
        P(seg, tile, None),
        P(),
        P(),
    )
    return jax.shard_map(
        shards,
        mesh=fine_mesh,
        in_specs=placed,
        out_specs=(P(axes, None), P(axes, None)),
        check_vma=False,
    )
```

```python
import functools
import math

import jax
import jax.numpy as jnp
import ml_dtypes
import numpy as np
from jax import lax
from jax.experimental import pallas as pl
from jax.experimental.pallas import tpu as pltpu
from jax.sharding import PartitionSpec as P

SEGS = 24
TV = 64
DEVICES = 256
TILES = 1024
BLOCKS = 8
SPAN = TILES // BLOCKS
LANES = 2 * TV
SAME_CORE = ("y", "x", "z_lo", "z_hi")

ridge_weight = 0.25
half_root = math.sqrt(0.5)


def split_constant(matrix):
    high = matrix.astype(np.float32).astype(ml_dtypes.bfloat16)
    low = (matrix - high.astype(np.float64)).astype(np.float32).astype(ml_dtypes.bfloat16)
    return high, low


def complex_block(real, imag):
    return np.block([[real, -imag], [imag, real]])


def transform_constants():
    steps = np.arange(SPAN)
    row = np.exp(-2j * np.pi * (np.outer(steps, steps) % SPAN) / SPAN)
    row_ahead = complex_block(row.real, row.imag)
    row_back = complex_block(row.real, -row.imag)
    steps = np.arange(TV)
    column = np.exp(-2j * np.pi * (np.outer(steps, steps) % TV) / TV)
    column = np.kron(np.eye(2), column)
    column_ahead = complex_block(column.real, -column.imag)
    column_back = complex_block(column.real, column.imag)
    pieces = []
    for matrix in (row_ahead, row_back, column_ahead, column_back):
        pieces += split_constant(matrix)
    return np.concatenate(pieces, axis=1)


def split(value):
    high = value.astype(jnp.bfloat16)
    low = (value - high.astype(jnp.float32)).astype(jnp.bfloat16)
    return high, low


def four_point(real, imag):
    sum_a, dif_a = (real[0] + real[2], imag[0] + imag[2]), (real[0] - real[2], imag[0] - imag[2])
    sum_b, dif_b = (real[1] + real[3], imag[1] + imag[3]), (real[1] - real[3], imag[1] - imag[3])
    return (
        (sum_a[0] + sum_b[0], sum_a[1] + sum_b[1]),
        (dif_a[0] + dif_b[1], dif_a[1] - dif_b[0]),
        (sum_a[0] - sum_b[0], sum_a[1] - sum_b[1]),
        (dif_a[0] - dif_b[1], dif_a[1] + dif_b[0]),
    )


def eight_point(real, imag):
    even = four_point([real[j] + real[j + 4] for j in range(4)], [imag[j] + imag[j + 4] for j in range(4)])
    dif_real = [real[j] - real[j + 4] for j in range(4)]
    dif_imag = [imag[j] - imag[j + 4] for j in range(4)]
    odd = four_point(
        [
            dif_real[0],
            (dif_real[1] + dif_imag[1]) * half_root,
            dif_imag[2],
            (dif_imag[3] - dif_real[3]) * half_root,
        ],
        [
            dif_imag[0],
            (dif_imag[1] - dif_real[1]) * half_root,
            -dif_real[2],
            (dif_real[3] + dif_imag[3]) * -half_root,
        ],
    )
    return [even[0], odd[0], even[1], odd[1], even[2], odd[2], even[3], odd[3]]


def table_parts(tables_ref):
    segments = (tables_ref.shape[0] - 2) // 3
    maps_ref = tables_ref.at[pl.ds(0, 2 * segments)]
    weights_ref = tables_ref.at[pl.ds(2 * segments, segments)]
    return maps_ref, weights_ref, tables_ref.at[pl.ds(3 * segments, 2)]


def cosine_sine(angle):
    turns = jnp.round(angle * (2.0 / math.pi))
    rest = angle - turns * 1.5703125
    rest = rest - turns * 4.837512969970703e-4
    rest = rest - turns * 7.549789948768648e-8
    square = rest * rest
    sine = rest + rest * square * (
        -1.6666654611e-1 + square * (8.3321608736e-3 + square * -1.9515295891e-4)
    )
    cosine = 1.0 - 0.5 * square + square * square * (
        4.166664568298827e-2 + square * (-1.388731625493765e-3 + square * 2.443315711809948e-5)
    )
    quarter = turns.astype(jnp.int32)
    swapped = (quarter & 1) == 1
    flip_cosine = ((quarter + 1) & 2) == 2
    flip_sine = (quarter & 2) == 2
    cosine, sine = jnp.where(swapped, sine, cosine), jnp.where(swapped, cosine, sine)
    return jnp.where(flip_cosine, -cosine, cosine), jnp.where(flip_sine, -sine, sine)


def prepare_kernel(
    first_ref, core_ref, sens_ref, field_ref, seg_map_ref, rows_ref, density_ref, tables_ref, core_out_ref
):
    core_out_ref[0] = core_ref[0]
    seg_local = rows_ref.shape[0]
    maps_ref, weights_ref, twist_ref = table_parts(tables_ref)
    lane = lax.broadcasted_iota(jnp.int32, (SPAN, LANES), 0).astype(jnp.float32)
    for block in range(BLOCKS):
        at = pl.ds(block * SPAN, SPAN)
        if block > 0:
            twist_cosine, twist_sine = cosine_sine(lane * (2.0 * math.pi * block / TILES))
            twist_ref[0, at, :] = twist_cosine
            twist_ref[1, at, :] = -twist_sine
        field = field_ref[:, at]
        field = jnp.concatenate([field, field], axis=0).T
        named = seg_map_ref[:, at]
        listed = []
        for local_seg in range(seg_local):
            member = jnp.where(named == first_ref[0] + local_seg, 1.0, 0.0)
            listed.append(jnp.where(jnp.sum(member, axis=0, keepdims=True) > 0.0, 1.0, 0.0))
        listed.append(jnp.zeros((8 - seg_local, SPAN), jnp.float32))
        listed = jnp.concatenate(listed, axis=0).T
        sens = [sens_ref[coil, at, :] for coil in range(2)]
        sens_real = jnp.concatenate([sens[0][:, :TV], sens[1][:, :TV]], axis=1)
        sens_imag = jnp.concatenate([sens[0][:, TV:], sens[1][:, TV:]], axis=1)
        for local_seg in range(seg_local):
            segment = first_ref[0] + local_seg
            seg_time = (segment.astype(jnp.float32) + 0.5) / SEGS
            cosine, sine = cosine_sine(field * seg_time)
            live = listed[:, local_seg : local_seg + 1]
            cosine, sine = cosine * live, sine * live
            maps_ref[2 * local_seg, at, :] = sens_real * cosine + sens_imag * sine
            maps_ref[2 * local_seg + 1, at, :] = sens_imag * cosine - sens_real * sine
    for local_seg in range(seg_local):
        rows_here = rows_ref[local_seg : local_seg + 1, :]
        high, low = split(density_ref[local_seg])
        pieces = jnp.concatenate([high, high, low, low], axis=0)
        for block in range(BLOCKS):
            grid_rows = lax.broadcasted_iota(jnp.int32, (SPAN, rows_here.shape[1]), 0) * BLOCKS + block
            chosen = jnp.where(grid_rows == rows_here, 1.0, 0.0).astype(jnp.bfloat16)
            summed = lax.dot_general(
                chosen, pieces, (((1,), (1,)), ((), ())), preferred_element_type=jnp.float32
            )
            weights_ref[local_seg, pl.ds(block * SPAN, SPAN), :] = (
                summed[:, :LANES] + summed[:, LANES:]
            ) * (1.0 / (TILES * TV))


def share_kernel(parts_ref, out_ref):
    value = jnp.sum(parts_ref[...], axis=0)
    for copy in range(out_ref.shape[0]):
        out_ref[copy] = value


def update_kernel(alpha_ref, beta_ref, parts_ref, right_ref, own_ref, solution_ref, residual_ref):
    eight = jnp.sum(parts_ref[...], axis=0)
    own_rows = right_ref.shape[0]
    last_sum = eight[:own_rows] + eight[own_rows:]
    right = right_ref[...]
    residual = right - alpha_ref[0] * (own_ref[...] + ridge_weight * right)
    direction = residual + beta_ref[0] * right
    solution_ref[...] = alpha_ref[0] * right + alpha_ref[1] * direction
    residual_ref[...] = residual - alpha_ref[1] * (last_sum + ridge_weight * direction)


CHUNK = 16


def normal_kernel(further, core_ref, *refs):
    if further:
        alpha_ref, beta_ref, mine_ref, other_ref, mine_sum_ref, other_sum_ref = refs[:6]
        refs = refs[6:]
    else:
        mine_ref, other_ref = refs[:2]
        refs = refs[2:]
    tables_ref, transforms_ref = refs[:2]
    keep_ref, send_ref, dir_dup, turned, left, left_back, right, back, total = refs[2:]
    maps_ref, weights_ref, twist_ref = table_parts(tables_ref)
    segments = weights_ref.shape[0]

    def transform(which, axis):
        high = transforms_ref[:, pl.ds(4 * SPAN * which, 2 * SPAN)]
        low = transforms_ref[:, pl.ds(4 * SPAN * which + 2 * SPAN, 2 * SPAN)]
        return jnp.concatenate([high, low, high] if axis == 1 else [high, high, low], axis=axis)

    core = core_ref[0]
    first_half = lax.broadcasted_iota(jnp.int32, (SPAN, LANES), 1) < TV
    for pair in range(BLOCKS // 2):
        for whose in range(2):
            from_rows = pl.ds(pair * SPAN, SPAN)
            to_rows = pl.ds((2 * pair + (core if whose == 0 else 1 - core)) * SPAN, SPAN)
            direction = (mine_ref, other_ref)[whose][from_rows, :]
            if further:
                image = (mine_sum_ref, other_sum_ref)[whose][from_rows, :] + ridge_weight * direction
                direction = direction - alpha_ref[0] * image + beta_ref[0] * direction
            rolled = pltpu.roll(direction, TV, 1)
            dir_dup[0, to_rows, :] = jnp.where(first_half, direction, rolled)
            dir_dup[1, to_rows, :] = jnp.where(first_half, rolled, direction)
    for segment in range(segments):
        for chunk in range(SPAN // CHUNK):
            at = [pl.ds(block * SPAN + chunk * CHUNK, CHUNK) for block in range(BLOCKS)]
            real, imag = [], []
            for rows in at:
                map_real, map_imag = maps_ref[2 * segment, rows, :], maps_ref[2 * segment + 1, rows, :]
                dir_real, dir_imag = dir_dup[0, rows, :], dir_dup[1, rows, :]
                real.append(map_real * dir_real - map_imag * dir_imag)
                imag.append(map_real * dir_imag + map_imag * dir_real)
            for block, (value_real, value_imag) in enumerate(eight_point(real, imag)):
                if block > 0:
                    twist_real, twist_imag = twist_ref[0, at[block], :], twist_ref[1, at[block], :]
                    value_real, value_imag = (
                        value_real * twist_real - value_imag * twist_imag,
                        value_real * twist_imag + value_imag * twist_real,
                    )
                lanes = pl.ds(block * LANES, LANES)
                for part, value in enumerate((value_real, value_imag)):
                    high, low = split(value)
                    start = part * SPAN + chunk * CHUNK
                    turned[pl.ds(start, CHUNK), lanes] = high
                    turned[pl.ds(2 * SPAN + start, CHUNK), lanes] = high
                    turned[pl.ds(4 * SPAN + start, CHUNK), lanes] = low
        for pair in range(BLOCKS // 2):
            grid = jnp.dot(
                transform(0, 1), turned[:, pl.ds(pair * 2 * LANES, 2 * LANES)], preferred_element_type=jnp.float32
            )
            for side in range(2):
                rows = pl.ds((2 * pair + side) * SPAN, SPAN)
                for part in range(2):
                    high, low = split(grid[part * SPAN : (part + 1) * SPAN, side * LANES : (side + 1) * LANES])
                    left[rows, pl.ds(part * LANES, LANES)] = high
                    left[rows, pl.ds((2 + part) * LANES, LANES)] = low
                    left[rows, pl.ds((4 + part) * LANES, LANES)] = high
        for pair in range(BLOCKS // 2):
            rows = pl.ds(pair * 2 * SPAN, 2 * SPAN)
            kspace = jnp.dot(left[rows, :], transform(2, 0), preferred_element_type=jnp.float32)
            weights = weights_ref[segment, rows, :]
            high, low = split(kspace * jnp.concatenate([weights, weights], axis=1))
            left_back[rows, pl.ds(0, 2 * LANES)] = high
            left_back[rows, pl.ds(2 * LANES, 2 * LANES)] = low
            left_back[rows, pl.ds(4 * LANES, 2 * LANES)] = high
        for pair in range(BLOCKS // 2):
            rows = pl.ds(pair * 2 * SPAN, 2 * SPAN)
            grid = jnp.dot(left_back[rows, :], transform(3, 0), preferred_element_type=jnp.float32)
            high, low = split(grid)
            for side in range(2):
                lanes = pl.ds((2 * pair + side) * LANES, LANES)
                for part in range(2):
                    piece = (slice(side * SPAN, (side + 1) * SPAN), slice(part * LANES, (part + 1) * LANES))
                    right[pl.ds(part * SPAN, SPAN), lanes] = high[piece]
                    right[pl.ds((2 + part) * SPAN, SPAN), lanes] = high[piece]
                    right[pl.ds((4 + part) * SPAN, SPAN), lanes] = low[piece]
        for pair in range(BLOCKS // 2):
            lanes = pl.ds(pair * 2 * LANES, 2 * LANES)
            back[:, lanes] = jnp.dot(transform(1, 1), right[:, lanes], preferred_element_type=jnp.float32)
        for chunk in range(SPAN // CHUNK):
            real, imag = [], []
            for block in range(BLOCKS):
                lanes = pl.ds(block * LANES, LANES)
                value_real = back[pl.ds(chunk * CHUNK, CHUNK), lanes]
                value_imag = back[pl.ds(SPAN + chunk * CHUNK, CHUNK), lanes]
                if block > 0:
                    rows = pl.ds(block * SPAN + chunk * CHUNK, CHUNK)
                    twist_real, twist_imag = twist_ref[0, rows, :], twist_ref[1, rows, :]
                    value_real, value_imag = (
                        value_real * twist_real + value_imag * twist_imag,
                        value_imag * twist_real - value_real * twist_imag,
                    )
                real.append(value_real)
                imag.append(value_imag)
            for block, (value_imag, value_real) in enumerate(eight_point(imag, real)):
                rows = pl.ds(block * SPAN + chunk * CHUNK, CHUNK)
                map_real, map_imag = maps_ref[2 * segment, rows, :], maps_ref[2 * segment + 1, rows, :]
                add_real = map_real * value_real + map_imag * value_imag
                add_imag = map_real * value_imag - map_imag * value_real
                if segment > 0:
                    add_real += total[0, rows, :]
                    add_imag += total[1, rows, :]
                total[0, rows, :] = add_real
                total[1, rows, :] = add_imag
    for pair in range(BLOCKS // 2):
        for whose, out_ref in enumerate((keep_ref, send_ref)):
            rows = pl.ds((2 * pair + (core if whose == 0 else 1 - core)) * SPAN, SPAN)
            real, imag = total[0, rows, :], total[1, rows, :]
            out_ref[pl.ds(pair * SPAN, SPAN), :] = jnp.where(
                first_half, real + pltpu.roll(real, TV, 1), imag + pltpu.roll(imag, TV, 1)
            )


def specs(scalars, arrays, in_place=0):
    return (
        [pl.BlockSpec(memory_space=pltpu.SMEM)] * scalars
        + [pl.BlockSpec(memory_space=pltpu.VMEM)] * arrays
        + [pl.BlockSpec(memory_space=pl.ANY)] * in_place
    )


def limit(mebibytes):
    return pltpu.CompilerParams(vmem_limit_bytes=mebibytes << 20)


def prepare(first_segment, core, sensitivity, field_map, seg_map, sample_rows, density):
    seg_local, samples = sample_rows.shape
    return pl.pallas_call(
        prepare_kernel,
        out_shape=(
            jax.ShapeDtypeStruct((3 * seg_local + 2, TILES, LANES), jnp.float32),
            jax.ShapeDtypeStruct((1,), jnp.int32),
        ),
        in_specs=specs(2, 5),
        out_specs=(specs(0, 1)[0], specs(1, 0)[0]),
        compiler_params=limit(8),
        cost_estimate=pl.CostEstimate(
            flops=2 * seg_local * TILES * samples * 2 * LANES,
            transcendentals=2 * seg_local * TILES * LANES,
            bytes_accessed=4 * seg_local * (3 * TILES * LANES + samples * TV) + 8 * TILES * LANES,
        ),
        name="maps_and_weights",
    )(first_segment, core, sensitivity, field_map, seg_map, sample_rows, density)


def apply_normal(core, steps, directions, tables):
    half = jax.ShapeDtypeStruct((TILES // 2, LANES), jnp.float32)
    segments = (tables[0].shape[0] - 2) // 3
    return pl.pallas_call(
        functools.partial(normal_kernel, len(steps) > 0),
        out_shape=(half, half),
        in_specs=specs(1 + len(steps), len(directions) + len(tables)),
        out_specs=tuple(specs(0, 2)),
        scratch_shapes=[
            pltpu.VMEM((2, TILES, LANES), jnp.float32),
            pltpu.VMEM((6 * SPAN, BLOCKS * LANES), jnp.bfloat16),
            pltpu.VMEM((TILES, 6 * LANES), jnp.bfloat16),
            pltpu.VMEM((TILES, 6 * LANES), jnp.bfloat16),
            pltpu.VMEM((6 * SPAN, BLOCKS * LANES), jnp.bfloat16),
            pltpu.VMEM((2 * SPAN, BLOCKS * LANES), jnp.float32),
            pltpu.VMEM((2, TILES, LANES), jnp.float32),
        ],
        compiler_params=limit(20),
        cost_estimate=pl.CostEstimate(
            flops=12 * segments * TILES * 6 * LANES * 4 * LANES,
            transcendentals=0,
            bytes_accessed=4 * segments * 4 * TILES * LANES,
        ),
        name="apply_normal",
    )(core, *steps, *directions, *tables)


def swap_cores(value):
    return lax.ppermute(value, "core", [(0, 1), (1, 0)])


def exchange(value, axes):
    return lax.all_to_all(value, axes, 0, 0, tiled=True)


def share(parts, count, copies):
    rows = parts.shape[0] // count
    shared = pl.pallas_call(
        share_kernel,
        out_shape=jax.ShapeDtypeStruct((copies, rows, LANES), jnp.float32),
        in_specs=specs(0, 1),
        out_specs=specs(0, 1)[0],
        compiler_params=limit(2),
        name="sum_and_copy",
    )(parts.reshape(count, rows, LANES))
    return shared.reshape(copies * rows, LANES)


def sum_to_owners(keep, send):
    return exchange(keep + swap_cores(send), SAME_CORE)


def sum_for_all(keep, send):
    copies = share(exchange(keep + swap_cores(send), ("y", "x")), 16, 8)
    copies = share(exchange(copies, ("z_lo", "z_hi")), 8, 16)
    mine = exchange(copies, ("y", "x"))
    return mine, swap_cores(mine)


def update(step_alpha, step_beta, parts, right_side, own_sum):
    own = jax.ShapeDtypeStruct(right_side.shape, jnp.float32)
    return pl.pallas_call(
        update_kernel,
        out_shape=(own, own),
        in_specs=specs(2, 3),
        out_specs=tuple(specs(0, 2)),
        compiler_params=limit(2),
        name="last_update",
    )(step_alpha, step_beta, parts.reshape(-1, 2 * right_side.shape[0], LANES), right_side, own_sum)


def shards(
    right_side, sensitivity, field_map, seg_map, sample_rows, density, step_alpha, step_beta
):
    seg_local = sample_rows.shape[0]
    first_segment = lax.axis_index(("y", "core")) * seg_local
    core = lax.axis_index("core").reshape(1)
    mine = exchange(jnp.tile(right_side, (DEVICES // 2, 1)), SAME_CORE)
    tables, core = prepare(
        first_segment.reshape(1),
        core,
        sensitivity,
        field_map.T,
        seg_map.T,
        sample_rows,
        jnp.swapaxes(density, 1, 2),
    )
    mine, core = lax.optimization_barrier((mine, core))
    gathered = (mine, swap_cores(mine))
    tables = (tables, jnp.asarray(transform_constants()))
    sums = sum_for_all(*apply_normal(core, (), gathered, tables))
    own_tiles = right_side.shape[0]
    own_start = lax.axis_index(SAME_CORE) * own_tiles
    own_sum = lax.dynamic_slice_in_dim(sums[0], own_start, own_tiles, 0)
    parts = sum_to_owners(
        *apply_normal(core, (step_alpha, step_beta), (*gathered, *sums), tables)
    )
    return update(step_alpha, step_beta, parts, right_side, own_sum)


def solution(mesh):
    axes = ("y", "core", "x", "z_lo", "z_hi")
    fine_mesh = jax.sharding.Mesh(mesh.devices.reshape(4, 2, 4, 4, 2), axes)
    seg, coil, tile = ("y", "core"), ("x", "z_lo"), "z_hi"
    placed = (
        P(axes, None),
        P(coil, None, None),
        P(),
        P(),
        P(seg, tile),
        P(seg, tile, None),
        P(),
        P(),
    )
    return jax.shard_map(
        shards,
        mesh=fine_mesh,
        in_specs=placed,
        out_specs=(P(axes, None), P(axes, None)),
        check_vma=False,
    )
```

```python
import functools
import math

import jax
import jax.numpy as jnp
import ml_dtypes
import numpy as np
from jax import lax
from jax.experimental import pallas as pl
from jax.experimental.pallas import tpu as pltpu
from jax.sharding import PartitionSpec as P

SEGS = 24
TV = 64
DEVICES = 256
TILES = 1024
BLOCKS = 8
SPAN = TILES // BLOCKS
LANES = 2 * TV
SAME_CORE = ("y", "x", "z_lo", "z_hi")

ridge_weight = 0.25
half_root = math.sqrt(0.5)


def split_constant(matrix):
    high = matrix.astype(np.float32).astype(ml_dtypes.bfloat16)
    low = (matrix - high.astype(np.float64)).astype(np.float32).astype(ml_dtypes.bfloat16)
    return high, low


def complex_block(real, imag):
    return np.block([[real, -imag], [imag, real]])


def transform_constants():
    steps = np.arange(SPAN)
    row = np.exp(-2j * np.pi * (np.outer(steps, steps) % SPAN) / SPAN)
    row_ahead = complex_block(row.real, row.imag)
    row_back = complex_block(row.real, -row.imag)
    steps = np.arange(TV)
    column = np.exp(-2j * np.pi * (np.outer(steps, steps) % TV) / TV)
    column = np.kron(np.eye(2), column)
    column_ahead = complex_block(column.real, -column.imag)
    column_back = complex_block(column.real, column.imag)
    pieces = []
    for matrix in (row_ahead, row_back, column_ahead, column_back):
        pieces += split_constant(matrix)
    return np.concatenate(pieces, axis=1)


def split(value):
    high = value.astype(jnp.bfloat16)
    low = (value - high.astype(jnp.float32)).astype(jnp.bfloat16)
    return high, low


def four_point(real, imag):
    sum_a, dif_a = (real[0] + real[2], imag[0] + imag[2]), (real[0] - real[2], imag[0] - imag[2])
    sum_b, dif_b = (real[1] + real[3], imag[1] + imag[3]), (real[1] - real[3], imag[1] - imag[3])
    return (
        (sum_a[0] + sum_b[0], sum_a[1] + sum_b[1]),
        (dif_a[0] + dif_b[1], dif_a[1] - dif_b[0]),
        (sum_a[0] - sum_b[0], sum_a[1] - sum_b[1]),
        (dif_a[0] - dif_b[1], dif_a[1] + dif_b[0]),
    )


def eight_point(real, imag):
    even = four_point([real[j] + real[j + 4] for j in range(4)], [imag[j] + imag[j + 4] for j in range(4)])
    dif_real = [real[j] - real[j + 4] for j in range(4)]
    dif_imag = [imag[j] - imag[j + 4] for j in range(4)]
    odd = four_point(
        [
            dif_real[0],
            (dif_real[1] + dif_imag[1]) * half_root,
            dif_imag[2],
            (dif_imag[3] - dif_real[3]) * half_root,
        ],
        [
            dif_imag[0],
            (dif_imag[1] - dif_real[1]) * half_root,
            -dif_real[2],
            (dif_real[3] + dif_imag[3]) * -half_root,
        ],
    )
    return [even[0], odd[0], even[1], odd[1], even[2], odd[2], even[3], odd[3]]


def table_parts(tables_ref):
    segments = (tables_ref.shape[0] - 2) // 3
    maps_ref = tables_ref.at[pl.ds(0, 2 * segments)]
    weights_ref = tables_ref.at[pl.ds(2 * segments, segments)]
    return maps_ref, weights_ref, tables_ref.at[pl.ds(3 * segments, 2)]


def cosine_sine(angle):
    turns = jnp.round(angle * (2.0 / math.pi))
    rest = angle - turns * 1.5703125
    rest = rest - turns * 4.837512969970703e-4
    rest = rest - turns * 7.549789948768648e-8
    square = rest * rest
    sine = rest + rest * square * (
        -1.6666654611e-1 + square * (8.3321608736e-3 + square * -1.9515295891e-4)
    )
    cosine = 1.0 - 0.5 * square + square * square * (
        4.166664568298827e-2 + square * (-1.388731625493765e-3 + square * 2.443315711809948e-5)
    )
    quarter = turns.astype(jnp.int32)
    swapped = (quarter & 1) == 1
    flip_cosine = ((quarter + 1) & 2) == 2
    flip_sine = (quarter & 2) == 2
    cosine, sine = jnp.where(swapped, sine, cosine), jnp.where(swapped, cosine, sine)
    return jnp.where(flip_cosine, -cosine, cosine), jnp.where(flip_sine, -sine, sine)


def prepare_kernel(
    first_ref, core_ref, sens_ref, field_ref, seg_map_ref, rows_ref, density_ref, tables_ref, core_out_ref
):
    core_out_ref[0] = core_ref[0]
    seg_local = rows_ref.shape[0]
    maps_ref, weights_ref, twist_ref = table_parts(tables_ref)
    lane = lax.broadcasted_iota(jnp.int32, (BLOCKS, SPAN), 1).astype(jnp.float32)
    turn = lax.broadcasted_iota(jnp.int32, (BLOCKS, SPAN), 0).astype(jnp.float32)
    twist_cosine, twist_sine = cosine_sine(lane * turn * (2.0 * math.pi / TILES))
    for block in range(BLOCKS):
        at = pl.ds(block * SPAN, SPAN)
        for part, value in enumerate((twist_cosine, -twist_sine)):
            twist_ref[part, at, :] = jnp.broadcast_to(value[block : block + 1, :], (LANES, SPAN)).T
        field = field_ref[:, at]
        field = jnp.concatenate([field, field], axis=0).T
        named = seg_map_ref[:, at]
        listed = []
        for local_seg in range(seg_local):
            member = jnp.where(named == first_ref[0] + local_seg, 1.0, 0.0)
            listed.append(jnp.where(jnp.sum(member, axis=0, keepdims=True) > 0.0, 1.0, 0.0))
        listed.append(jnp.zeros((8 - seg_local, SPAN), jnp.float32))
        listed = jnp.concatenate(listed, axis=0).T
        sens = [sens_ref[coil, at, :] for coil in range(2)]
        sens_real = jnp.concatenate([sens[0][:, :TV], sens[1][:, :TV]], axis=1)
        sens_imag = jnp.concatenate([sens[0][:, TV:], sens[1][:, TV:]], axis=1)
        for local_seg in range(seg_local):
            segment = first_ref[0] + local_seg
            seg_time = (segment.astype(jnp.float32) + 0.5) / SEGS
            cosine, sine = cosine_sine(field * seg_time)
            live = listed[:, local_seg : local_seg + 1]
            cosine, sine = cosine * live, sine * live
            maps_ref[2 * local_seg, at, :] = sens_real * cosine + sens_imag * sine
            maps_ref[2 * local_seg + 1, at, :] = sens_imag * cosine - sens_real * sine
    for local_seg in range(seg_local):
        rows_here = rows_ref[local_seg : local_seg + 1, :]
        high, low = split(density_ref[local_seg])
        pieces = jnp.concatenate([high, high, low, low], axis=0)
        for block in range(BLOCKS):
            grid_rows = lax.broadcasted_iota(jnp.int32, (SPAN, rows_here.shape[1]), 0) * BLOCKS + block
            chosen = jnp.where(grid_rows == rows_here, 1.0, 0.0).astype(jnp.bfloat16)
            summed = lax.dot_general(
                chosen, pieces, (((1,), (1,)), ((), ())), preferred_element_type=jnp.float32
            )
            weights_ref[local_seg, pl.ds(block * SPAN, SPAN), :] = (
                summed[:, :LANES] + summed[:, LANES:]
            ) * (1.0 / (TILES * TV))


def share_kernel(parts_ref, out_ref):
    value = jnp.sum(parts_ref[...], axis=0)
    for copy in range(out_ref.shape[0]):
        out_ref[copy] = value


def update_kernel(alpha_ref, beta_ref, parts_ref, right_ref, own_ref, solution_ref, residual_ref):
    eight = jnp.sum(parts_ref[...], axis=0)
    own_rows = right_ref.shape[0]
    last_sum = eight[:own_rows] + eight[own_rows:]
    right = right_ref[...]
    residual = right - alpha_ref[0] * (own_ref[...] + ridge_weight * right)
    direction = residual + beta_ref[0] * right
    solution_ref[...] = alpha_ref[0] * right + alpha_ref[1] * direction
    residual_ref[...] = residual - alpha_ref[1] * (last_sum + ridge_weight * direction)


CHUNK = 16


def normal_kernel(further, core_ref, *refs):
    if further:
        alpha_ref, beta_ref, mine_ref, other_ref, mine_sum_ref, other_sum_ref = refs[:6]
        refs = refs[6:]
    else:
        mine_ref, other_ref = refs[:2]
        refs = refs[2:]
    tables_ref, transforms_ref = refs[:2]
    keep_ref, send_ref, dir_dup, turned, left, left_back, right, back, total = refs[2:]
    maps_ref, weights_ref, twist_ref = table_parts(tables_ref)
    segments = weights_ref.shape[0]

    def transform(which, axis):
        high = transforms_ref[:, pl.ds(4 * SPAN * which, 2 * SPAN)]
        low = transforms_ref[:, pl.ds(4 * SPAN * which + 2 * SPAN, 2 * SPAN)]
        return jnp.concatenate([high, low, high] if axis == 1 else [high, high, low], axis=axis)

    core = core_ref[0]
    first_half = lax.broadcasted_iota(jnp.int32, (SPAN, LANES), 1) < TV
    for pair in range(BLOCKS // 2):
        for whose in range(2):
            from_rows = pl.ds(pair * SPAN, SPAN)
            to_rows = pl.ds((2 * pair + (core if whose == 0 else 1 - core)) * SPAN, SPAN)
            direction = (mine_ref, other_ref)[whose][from_rows, :]
            if further:
                image = (mine_sum_ref, other_sum_ref)[whose][from_rows, :] + ridge_weight * direction
                direction = direction - alpha_ref[0] * image + beta_ref[0] * direction
            rolled = pltpu.roll(direction, TV, 1)
            dir_dup[0, to_rows, :] = jnp.where(first_half, direction, rolled)
            dir_dup[1, to_rows, :] = jnp.where(first_half, rolled, direction)
    for segment in range(segments):
        for chunk in range(SPAN // CHUNK):
            at = [pl.ds(block * SPAN + chunk * CHUNK, CHUNK) for block in range(BLOCKS)]
            real, imag = [], []
            for rows in at:
                map_real, map_imag = maps_ref[2 * segment, rows, :], maps_ref[2 * segment + 1, rows, :]
                dir_real, dir_imag = dir_dup[0, rows, :], dir_dup[1, rows, :]
                real.append(map_real * dir_real - map_imag * dir_imag)
                imag.append(map_real * dir_imag + map_imag * dir_real)
            for block, (value_real, value_imag) in enumerate(eight_point(real, imag)):
                if block > 0:
                    twist_real, twist_imag = twist_ref[0, at[block], :], twist_ref[1, at[block], :]
                    value_real, value_imag = (
                        value_real * twist_real - value_imag * twist_imag,
                        value_real * twist_imag + value_imag * twist_real,
                    )
                lanes = pl.ds(block * LANES, LANES)
                for part, value in enumerate((value_real, value_imag)):
                    high, low = split(value)
                    start = part * SPAN + chunk * CHUNK
                    turned[pl.ds(start, CHUNK), lanes] = high
                    turned[pl.ds(2 * SPAN + start, CHUNK), lanes] = high
                    turned[pl.ds(4 * SPAN + start, CHUNK), lanes] = low
        for pair in range(BLOCKS // 2):
            grid = jnp.dot(
                transform(0, 1), turned[:, pl.ds(pair * 2 * LANES, 2 * LANES)], preferred_element_type=jnp.float32
            )
            for side in range(2):
                rows = pl.ds((2 * pair + side) * SPAN, SPAN)
                for part in range(2):
                    high, low = split(grid[part * SPAN : (part + 1) * SPAN, side * LANES : (side + 1) * LANES])
                    left[rows, pl.ds(part * LANES, LANES)] = high
                    left[rows, pl.ds((2 + part) * LANES, LANES)] = low
                    left[rows, pl.ds((4 + part) * LANES, LANES)] = high
        for pair in range(BLOCKS // 2):
            rows = pl.ds(pair * 2 * SPAN, 2 * SPAN)
            kspace = jnp.dot(left[rows, :], transform(2, 0), preferred_element_type=jnp.float32)
            weights = weights_ref[segment, rows, :]
            high, low = split(kspace * jnp.concatenate([weights, weights], axis=1))
            left_back[rows, pl.ds(0, 2 * LANES)] = high
            left_back[rows, pl.ds(2 * LANES, 2 * LANES)] = low
            left_back[rows, pl.ds(4 * LANES, 2 * LANES)] = high
        for pair in range(BLOCKS // 2):
            rows = pl.ds(pair * 2 * SPAN, 2 * SPAN)
            grid = jnp.dot(left_back[rows, :], transform(3, 0), preferred_element_type=jnp.float32)
            high, low = split(grid)
            for side in range(2):
                lanes = pl.ds((2 * pair + side) * LANES, LANES)
                for part in range(2):
                    piece = (slice(side * SPAN, (side + 1) * SPAN), slice(part * LANES, (part + 1) * LANES))
                    right[pl.ds(part * SPAN, SPAN), lanes] = high[piece]
                    right[pl.ds((2 + part) * SPAN, SPAN), lanes] = high[piece]
                    right[pl.ds((4 + part) * SPAN, SPAN), lanes] = low[piece]
        for pair in range(BLOCKS // 2):
            lanes = pl.ds(pair * 2 * LANES, 2 * LANES)
            back[:, lanes] = jnp.dot(transform(1, 1), right[:, lanes], preferred_element_type=jnp.float32)
        for chunk in range(SPAN // CHUNK):
            real, imag = [], []
            for block in range(BLOCKS):
                lanes = pl.ds(block * LANES, LANES)
                value_real = back[pl.ds(chunk * CHUNK, CHUNK), lanes]
                value_imag = back[pl.ds(SPAN + chunk * CHUNK, CHUNK), lanes]
                if block > 0:
                    rows = pl.ds(block * SPAN + chunk * CHUNK, CHUNK)
                    twist_real, twist_imag = twist_ref[0, rows, :], twist_ref[1, rows, :]
                    value_real, value_imag = (
                        value_real * twist_real + value_imag * twist_imag,
                        value_imag * twist_real - value_real * twist_imag,
                    )
                real.append(value_real)
                imag.append(value_imag)
            for block, (value_imag, value_real) in enumerate(eight_point(imag, real)):
                rows = pl.ds(block * SPAN + chunk * CHUNK, CHUNK)
                map_real, map_imag = maps_ref[2 * segment, rows, :], maps_ref[2 * segment + 1, rows, :]
                add_real = map_real * value_real + map_imag * value_imag
                add_imag = map_real * value_imag - map_imag * value_real
                if segment > 0:
                    add_real += total[0, rows, :]
                    add_imag += total[1, rows, :]
                total[0, rows, :] = add_real
                total[1, rows, :] = add_imag
    for pair in range(BLOCKS // 2):
        for whose, out_ref in enumerate((keep_ref, send_ref)):
            rows = pl.ds((2 * pair + (core if whose == 0 else 1 - core)) * SPAN, SPAN)
            real, imag = total[0, rows, :], total[1, rows, :]
            out_ref[pl.ds(pair * SPAN, SPAN), :] = jnp.where(
                first_half, real + pltpu.roll(real, TV, 1), imag + pltpu.roll(imag, TV, 1)
            )


def specs(scalars, arrays, in_place=0):
    return (
        [pl.BlockSpec(memory_space=pltpu.SMEM)] * scalars
        + [pl.BlockSpec(memory_space=pltpu.VMEM)] * arrays
        + [pl.BlockSpec(memory_space=pl.ANY)] * in_place
    )


def limit(mebibytes):
    return pltpu.CompilerParams(vmem_limit_bytes=mebibytes << 20)


def prepare(first_segment, core, sensitivity, field_map, seg_map, sample_rows, density):
    seg_local, samples = sample_rows.shape
    return pl.pallas_call(
        prepare_kernel,
        out_shape=(
            jax.ShapeDtypeStruct((3 * seg_local + 2, TILES, LANES), jnp.float32),
            jax.ShapeDtypeStruct((1,), jnp.int32),
        ),
        in_specs=specs(2, 5),
        out_specs=(specs(0, 1)[0], specs(1, 0)[0]),
        compiler_params=limit(60),
        cost_estimate=pl.CostEstimate(
            flops=2 * seg_local * TILES * samples * 2 * LANES,
            transcendentals=2 * seg_local * TILES * LANES,
            bytes_accessed=4 * seg_local * (3 * TILES * LANES + samples * TV) + 8 * TILES * LANES,
        ),
        name="maps_and_weights",
    )(first_segment, core, sensitivity, field_map, seg_map, sample_rows, density)


def apply_normal(core, steps, directions, tables):
    half = jax.ShapeDtypeStruct((TILES // 2, LANES), jnp.float32)
    segments = (tables[0].shape[0] - 2) // 3
    return pl.pallas_call(
        functools.partial(normal_kernel, len(steps) > 0),
        out_shape=(half, half),
        in_specs=specs(1 + len(steps), len(directions) + len(tables)),
        out_specs=tuple(specs(0, 2)),
        scratch_shapes=[
            pltpu.VMEM((2, TILES, LANES), jnp.float32),
            pltpu.VMEM((6 * SPAN, BLOCKS * LANES), jnp.bfloat16),
            pltpu.VMEM((TILES, 6 * LANES), jnp.bfloat16),
            pltpu.VMEM((TILES, 6 * LANES), jnp.bfloat16),
            pltpu.VMEM((6 * SPAN, BLOCKS * LANES), jnp.bfloat16),
            pltpu.VMEM((2 * SPAN, BLOCKS * LANES), jnp.float32),
            pltpu.VMEM((2, TILES, LANES), jnp.float32),
        ],
        compiler_params=limit(20),
        cost_estimate=pl.CostEstimate(
            flops=12 * segments * TILES * 6 * LANES * 4 * LANES,
            transcendentals=0,
            bytes_accessed=4 * segments * 4 * TILES * LANES,
        ),
        name="apply_normal",
    )(core, *steps, *directions, *tables)


def swap_cores(value):
    return lax.ppermute(value, "core", [(0, 1), (1, 0)])


def exchange(value, axes):
    return lax.all_to_all(value, axes, 0, 0, tiled=True)


def share(parts, count, copies):
    rows = parts.shape[0] // count
    shared = pl.pallas_call(
        share_kernel,
        out_shape=jax.ShapeDtypeStruct((copies, rows, LANES), jnp.float32),
        in_specs=specs(0, 1),
        out_specs=specs(0, 1)[0],
        compiler_params=limit(2),
        name="sum_and_copy",
    )(parts.reshape(count, rows, LANES))
    return shared.reshape(copies * rows, LANES)


def sum_to_owners(keep, send):
    return exchange(keep + swap_cores(send), SAME_CORE)


def sum_for_all(keep, send):
    copies = share(exchange(keep + swap_cores(send), ("y", "x")), 16, 8)
    copies = share(exchange(copies, ("z_lo", "z_hi")), 8, 16)
    mine = exchange(copies, ("y", "x"))
    return mine, swap_cores(mine)


def update(step_alpha, step_beta, parts, right_side, own_sum):
    own = jax.ShapeDtypeStruct(right_side.shape, jnp.float32)
    return pl.pallas_call(
        update_kernel,
        out_shape=(own, own),
        in_specs=specs(2, 3),
        out_specs=tuple(specs(0, 2)),
        compiler_params=limit(2),
        name="last_update",
    )(step_alpha, step_beta, parts.reshape(-1, 2 * right_side.shape[0], LANES), right_side, own_sum)


def shards(
    right_side, sensitivity, field_map, seg_map, sample_rows, density, step_alpha, step_beta
):
    seg_local = sample_rows.shape[0]
    first_segment = lax.axis_index(("y", "core")) * seg_local
    core = lax.axis_index("core").reshape(1)
    mine = exchange(jnp.tile(right_side, (DEVICES // 2, 1)), SAME_CORE)
    tables, core = prepare(
        first_segment.reshape(1),
        core,
        sensitivity,
        field_map.T,
        seg_map.T,
        sample_rows,
        jnp.swapaxes(density, 1, 2),
    )
    mine, core = lax.optimization_barrier((mine, core))
    gathered = (mine, swap_cores(mine))
    tables = (tables, jnp.asarray(transform_constants()))
    sums = sum_for_all(*apply_normal(core, (), gathered, tables))
    own_tiles = right_side.shape[0]
    own_start = lax.axis_index(SAME_CORE) * own_tiles
    own_sum = lax.dynamic_slice_in_dim(sums[0], own_start, own_tiles, 0)
    parts = sum_to_owners(
        *apply_normal(core, (step_alpha, step_beta), (*gathered, *sums), tables)
    )
    return update(step_alpha, step_beta, parts, right_side, own_sum)


def solution(mesh):
    axes = ("y", "core", "x", "z_lo", "z_hi")
    fine_mesh = jax.sharding.Mesh(mesh.devices.reshape(4, 2, 4, 4, 2), axes)
    seg, coil, tile = ("y", "core"), ("x", "z_lo"), "z_hi"
    placed = (
        P(axes, None),
        P(coil, None, None),
        P(),
        P(),
        P(seg, tile),
        P(seg, tile, None),
        P(),
        P(),
    )
    return jax.shard_map(
        shards,
        mesh=fine_mesh,
        in_specs=placed,
        out_specs=(P(axes, None), P(axes, None)),
        check_vma=False,
    )
```

```python
import functools
import math

import jax
import jax.numpy as jnp
import ml_dtypes
import numpy as np
from jax import lax
from jax.experimental import pallas as pl
from jax.experimental.pallas import tpu as pltpu
from jax.sharding import PartitionSpec as P

SEGS = 24
TV = 64
DEVICES = 256
TILES = 1024
BLOCKS = 8
SPAN = TILES // BLOCKS
LANES = 2 * TV
SAME_CORE = ("y", "x", "z_lo", "z_hi")

ridge_weight = 0.25
half_root = math.sqrt(0.5)


def split_constant(matrix):
    high = matrix.astype(np.float32).astype(ml_dtypes.bfloat16)
    low = (matrix - high.astype(np.float64)).astype(np.float32).astype(ml_dtypes.bfloat16)
    return high, low


def complex_block(real, imag):
    return np.block([[real, -imag], [imag, real]])


def transform_constants():
    steps = np.arange(SPAN)
    row = np.exp(-2j * np.pi * (np.outer(steps, steps) % SPAN) / SPAN)
    row_ahead = complex_block(row.real, row.imag)
    row_back = complex_block(row.real, -row.imag)
    steps = np.arange(TV)
    column = np.exp(-2j * np.pi * (np.outer(steps, steps) % TV) / TV)
    column = np.kron(np.eye(2), column)
    column_ahead = complex_block(column.real, -column.imag)
    column_back = complex_block(column.real, column.imag)
    pieces = []
    for matrix in (row_ahead, row_back, column_ahead, column_back):
        pieces += split_constant(matrix)
    return np.concatenate(pieces, axis=1)


def split(value):
    high = value.astype(jnp.bfloat16)
    low = (value - high.astype(jnp.float32)).astype(jnp.bfloat16)
    return high, low


def four_point(real, imag):
    sum_a, dif_a = (real[0] + real[2], imag[0] + imag[2]), (real[0] - real[2], imag[0] - imag[2])
    sum_b, dif_b = (real[1] + real[3], imag[1] + imag[3]), (real[1] - real[3], imag[1] - imag[3])
    return (
        (sum_a[0] + sum_b[0], sum_a[1] + sum_b[1]),
        (dif_a[0] + dif_b[1], dif_a[1] - dif_b[0]),
        (sum_a[0] - sum_b[0], sum_a[1] - sum_b[1]),
        (dif_a[0] - dif_b[1], dif_a[1] + dif_b[0]),
    )


def eight_point(real, imag):
    even = four_point([real[j] + real[j + 4] for j in range(4)], [imag[j] + imag[j + 4] for j in range(4)])
    dif_real = [real[j] - real[j + 4] for j in range(4)]
    dif_imag = [imag[j] - imag[j + 4] for j in range(4)]
    odd = four_point(
        [
            dif_real[0],
            (dif_real[1] + dif_imag[1]) * half_root,
            dif_imag[2],
            (dif_imag[3] - dif_real[3]) * half_root,
        ],
        [
            dif_imag[0],
            (dif_imag[1] - dif_real[1]) * half_root,
            -dif_real[2],
            (dif_real[3] + dif_imag[3]) * -half_root,
        ],
    )
    return [even[0], odd[0], even[1], odd[1], even[2], odd[2], even[3], odd[3]]


def table_parts(tables_ref):
    segments = (tables_ref.shape[0] - 2) // 3
    maps_ref = tables_ref.at[pl.ds(0, 2 * segments)]
    weights_ref = tables_ref.at[pl.ds(2 * segments, segments)]
    return maps_ref, weights_ref, tables_ref.at[pl.ds(3 * segments, 2)]


def cosine_sine(angle):
    turns = jnp.round(angle * (2.0 / math.pi))
    rest = angle - turns * 1.5703125
    rest = rest - turns * 4.837512969970703e-4
    rest = rest - turns * 7.549789948768648e-8
    square = rest * rest
    sine = rest + rest * square * (
        -1.6666654611e-1 + square * (8.3321608736e-3 + square * -1.9515295891e-4)
    )
    cosine = 1.0 - 0.5 * square + square * square * (
        4.166664568298827e-2 + square * (-1.388731625493765e-3 + square * 2.443315711809948e-5)
    )
    quarter = turns.astype(jnp.int32)
    swapped = (quarter & 1) == 1
    flip_cosine = ((quarter + 1) & 2) == 2
    flip_sine = (quarter & 2) == 2
    cosine, sine = jnp.where(swapped, sine, cosine), jnp.where(swapped, cosine, sine)
    return jnp.where(flip_cosine, -cosine, cosine), jnp.where(flip_sine, -sine, sine)


def prepare_kernel(
    first_ref, core_ref, sens_ref, field_ref, seg_map_ref, rows_ref, density_ref, tables_ref, core_out_ref
):
    core_out_ref[0] = core_ref[0]
    seg_local = rows_ref.shape[0]
    maps_ref, weights_ref, twist_ref = table_parts(tables_ref)
    lane = lax.broadcasted_iota(jnp.int32, (BLOCKS, SPAN), 1).astype(jnp.float32)
    turn = lax.broadcasted_iota(jnp.int32, (BLOCKS, SPAN), 0).astype(jnp.float32)
    twist_cosine, twist_sine = cosine_sine(lane * turn * (2.0 * math.pi / TILES))
    for block in range(BLOCKS):
        at = pl.ds(block * SPAN, SPAN)
        for part, value in enumerate((twist_cosine, -twist_sine)):
            twist_ref[part, at, :] = jnp.broadcast_to(value[block : block + 1, :], (LANES, SPAN)).T
        field = field_ref[:, at]
        field = jnp.concatenate([field, field], axis=0).T
        named = seg_map_ref[:, at]
        listed = []
        for local_seg in range(seg_local):
            member = jnp.where(named == first_ref[0] + local_seg, 1.0, 0.0)
            listed.append(jnp.where(jnp.sum(member, axis=0, keepdims=True) > 0.0, 1.0, 0.0))
        listed.append(jnp.zeros((8 - seg_local, SPAN), jnp.float32))
        listed = jnp.concatenate(listed, axis=0).T
        sens = [sens_ref[coil, at, :] for coil in range(2)]
        sens_real = jnp.concatenate([sens[0][:, :TV], sens[1][:, :TV]], axis=1)
        sens_imag = jnp.concatenate([sens[0][:, TV:], sens[1][:, TV:]], axis=1)
        for local_seg in range(seg_local):
            segment = first_ref[0] + local_seg
            seg_time = (segment.astype(jnp.float32) + 0.5) / SEGS
            cosine, sine = cosine_sine(field * seg_time)
            live = listed[:, local_seg : local_seg + 1]
            cosine, sine = cosine * live, sine * live
            maps_ref[2 * local_seg, at, :] = sens_real * cosine + sens_imag * sine
            maps_ref[2 * local_seg + 1, at, :] = sens_imag * cosine - sens_real * sine
    for local_seg in range(seg_local):
        rows_here = rows_ref[local_seg : local_seg + 1, :]
        high, low = split(density_ref[local_seg])
        pieces = jnp.concatenate([high, high, low, low], axis=0)
        for block in range(BLOCKS):
            grid_rows = lax.broadcasted_iota(jnp.int32, (SPAN, rows_here.shape[1]), 0) * BLOCKS + block
            chosen = jnp.where(grid_rows == rows_here, 1.0, 0.0).astype(jnp.bfloat16)
            summed = lax.dot_general(
                chosen, pieces, (((1,), (1,)), ((), ())), preferred_element_type=jnp.float32
            )
            weights_ref[local_seg, pl.ds(block * SPAN, SPAN), :] = (
                summed[:, :LANES] + summed[:, LANES:]
            ) * (1.0 / (TILES * TV))


def share_kernel(parts_ref, out_ref):
    value = jnp.sum(parts_ref[...], axis=0)
    for copy in range(out_ref.shape[0]):
        out_ref[copy] = value


def update_kernel(alpha_ref, beta_ref, parts_ref, right_ref, own_ref, solution_ref, residual_ref):
    eight = jnp.sum(parts_ref[...], axis=0)
    own_rows = right_ref.shape[0]
    last_sum = eight[:own_rows] + eight[own_rows:]
    right = right_ref[...]
    residual = right - alpha_ref[0] * (own_ref[...] + ridge_weight * right)
    direction = residual + beta_ref[0] * right
    solution_ref[...] = alpha_ref[0] * right + alpha_ref[1] * direction
    residual_ref[...] = residual - alpha_ref[1] * (last_sum + ridge_weight * direction)


CHUNK = 16


def normal_kernel(further, core_ref, *refs):
    if further:
        alpha_ref, beta_ref, mine_ref, other_ref, mine_sum_ref, other_sum_ref = refs[:6]
        refs = refs[6:]
    else:
        mine_ref, other_ref = refs[:2]
        refs = refs[2:]
    tables_ref, transforms_ref = refs[:2]
    keep_ref, send_ref, dir_dup, turned, left, left_back, right, back, total = refs[2:]
    maps_ref, weights_ref, twist_ref = table_parts(tables_ref)
    segments = weights_ref.shape[0]

    def three_passes(which, data, data_left):
        matrix_high = transforms_ref[:, pl.ds(4 * SPAN * which, 2 * SPAN)]
        matrix_low = transforms_ref[:, pl.ds(4 * SPAN * which + 2 * SPAN, 2 * SPAN)]

        def product(matrix, value):
            pair = (value, matrix) if data_left else (matrix, value)
            return jnp.dot(*pair, preferred_element_type=jnp.float32)

        high, low = data
        return product(matrix_high, high) + product(matrix_low, high) + product(matrix_high, low)

    def halves(ref, index, axis):
        half = ref.shape[axis] // 2
        if axis == 0:
            return ref[pl.ds(0, half), index], ref[pl.ds(half, half), index]
        return ref[index, pl.ds(0, half)], ref[index, pl.ds(half, half)]

    core = core_ref[0]
    first_half = lax.broadcasted_iota(jnp.int32, (SPAN, LANES), 1) < TV
    for pair in range(BLOCKS // 2):
        for whose in range(2):
            from_rows = pl.ds(pair * SPAN, SPAN)
            to_rows = pl.ds((2 * pair + (core if whose == 0 else 1 - core)) * SPAN, SPAN)
            direction = (mine_ref, other_ref)[whose][from_rows, :]
            if further:
                image = (mine_sum_ref, other_sum_ref)[whose][from_rows, :] + ridge_weight * direction
                direction = direction - alpha_ref[0] * image + beta_ref[0] * direction
            rolled = pltpu.roll(direction, TV, 1)
            dir_dup[0, to_rows, :] = jnp.where(first_half, direction, rolled)
            dir_dup[1, to_rows, :] = jnp.where(first_half, rolled, direction)
    for segment in range(segments):
        for chunk in range(SPAN // CHUNK):
            at = [pl.ds(block * SPAN + chunk * CHUNK, CHUNK) for block in range(BLOCKS)]
            real, imag = [], []
            for rows in at:
                map_real, map_imag = maps_ref[2 * segment, rows, :], maps_ref[2 * segment + 1, rows, :]
                dir_real, dir_imag = dir_dup[0, rows, :], dir_dup[1, rows, :]
                real.append(map_real * dir_real - map_imag * dir_imag)
                imag.append(map_real * dir_imag + map_imag * dir_real)
            for block, (value_real, value_imag) in enumerate(eight_point(real, imag)):
                if block > 0:
                    twist_real, twist_imag = twist_ref[0, at[block], :], twist_ref[1, at[block], :]
                    value_real, value_imag = (
                        value_real * twist_real - value_imag * twist_imag,
                        value_real * twist_imag + value_imag * twist_real,
                    )
                lanes = pl.ds(block * LANES, LANES)
                for part, value in enumerate((value_real, value_imag)):
                    high, low = split(value)
                    start = part * SPAN + chunk * CHUNK
                    turned[pl.ds(start, CHUNK), lanes] = high
                    turned[pl.ds(2 * SPAN + start, CHUNK), lanes] = low
        for pair in range(BLOCKS // 2):
            grid = three_passes(0, halves(turned, pl.ds(pair * 2 * LANES, 2 * LANES), 0), False)
            for side in range(2):
                rows = pl.ds((2 * pair + side) * SPAN, SPAN)
                for part in range(2):
                    high, low = split(grid[part * SPAN : (part + 1) * SPAN, side * LANES : (side + 1) * LANES])
                    left[rows, pl.ds(part * LANES, LANES)] = high
                    left[rows, pl.ds((2 + part) * LANES, LANES)] = low
        for pair in range(BLOCKS // 2):
            rows = pl.ds(pair * 2 * SPAN, 2 * SPAN)
            kspace = three_passes(2, halves(left, rows, 1), True)
            weights = weights_ref[segment, rows, :]
            high, low = split(kspace * jnp.concatenate([weights, weights], axis=1))
            left_back[rows, pl.ds(0, 2 * LANES)] = high
            left_back[rows, pl.ds(2 * LANES, 2 * LANES)] = low
        for pair in range(BLOCKS // 2):
            rows = pl.ds(pair * 2 * SPAN, 2 * SPAN)
            grid = three_passes(3, halves(left_back, rows, 1), True)
            high, low = split(grid)
            for side in range(2):
                lanes = pl.ds((2 * pair + side) * LANES, LANES)
                for part in range(2):
                    piece = (slice(side * SPAN, (side + 1) * SPAN), slice(part * LANES, (part + 1) * LANES))
                    right[pl.ds(part * SPAN, SPAN), lanes] = high[piece]
                    right[pl.ds((2 + part) * SPAN, SPAN), lanes] = low[piece]
        for pair in range(BLOCKS // 2):
            lanes = pl.ds(pair * 2 * LANES, 2 * LANES)
            back[:, lanes] = three_passes(1, halves(right, lanes, 0), False)
        for chunk in range(SPAN // CHUNK):
            real, imag = [], []
            for block in range(BLOCKS):
                lanes = pl.ds(block * LANES, LANES)
                value_real = back[pl.ds(chunk * CHUNK, CHUNK), lanes]
                value_imag = back[pl.ds(SPAN + chunk * CHUNK, CHUNK), lanes]
                if block > 0:
                    rows = pl.ds(block * SPAN + chunk * CHUNK, CHUNK)
                    twist_real, twist_imag = twist_ref[0, rows, :], twist_ref[1, rows, :]
                    value_real, value_imag = (
                        value_real * twist_real + value_imag * twist_imag,
                        value_imag * twist_real - value_real * twist_imag,
                    )
                real.append(value_real)
                imag.append(value_imag)
            for block, (value_imag, value_real) in enumerate(eight_point(imag, real)):
                rows = pl.ds(block * SPAN + chunk * CHUNK, CHUNK)
                map_real, map_imag = maps_ref[2 * segment, rows, :], maps_ref[2 * segment + 1, rows, :]
                add_real = map_real * value_real + map_imag * value_imag
                add_imag = map_real * value_imag - map_imag * value_real
                if segment > 0:
                    add_real += total[0, rows, :]
                    add_imag += total[1, rows, :]
                total[0, rows, :] = add_real
                total[1, rows, :] = add_imag
    for pair in range(BLOCKS // 2):
        for whose, out_ref in enumerate((keep_ref, send_ref)):
            rows = pl.ds((2 * pair + (core if whose == 0 else 1 - core)) * SPAN, SPAN)
            real, imag = total[0, rows, :], total[1, rows, :]
            out_ref[pl.ds(pair * SPAN, SPAN), :] = jnp.where(
                first_half, real + pltpu.roll(real, TV, 1), imag + pltpu.roll(imag, TV, 1)
            )


def specs(scalars, arrays, in_place=0):
    return (
        [pl.BlockSpec(memory_space=pltpu.SMEM)] * scalars
        + [pl.BlockSpec(memory_space=pltpu.VMEM)] * arrays
        + [pl.BlockSpec(memory_space=pl.ANY)] * in_place
    )


def limit(mebibytes):
    return pltpu.CompilerParams(vmem_limit_bytes=mebibytes << 20)


def prepare(first_segment, core, sensitivity, field_map, seg_map, sample_rows, density):
    seg_local, samples = sample_rows.shape
    return pl.pallas_call(
        prepare_kernel,
        out_shape=(
            jax.ShapeDtypeStruct((3 * seg_local + 2, TILES, LANES), jnp.float32),
            jax.ShapeDtypeStruct((1,), jnp.int32),
        ),
        in_specs=specs(2, 5),
        out_specs=(specs(0, 1)[0], specs(1, 0)[0]),
        compiler_params=limit(60),
        cost_estimate=pl.CostEstimate(
            flops=2 * seg_local * TILES * samples * 2 * LANES,
            transcendentals=2 * seg_local * TILES * LANES,
            bytes_accessed=4 * seg_local * (3 * TILES * LANES + samples * TV) + 8 * TILES * LANES,
        ),
        name="maps_and_weights",
    )(first_segment, core, sensitivity, field_map, seg_map, sample_rows, density)


def apply_normal(core, steps, directions, tables):
    half = jax.ShapeDtypeStruct((TILES // 2, LANES), jnp.float32)
    segments = (tables[0].shape[0] - 2) // 3
    return pl.pallas_call(
        functools.partial(normal_kernel, len(steps) > 0),
        out_shape=(half, half),
        in_specs=specs(1 + len(steps), len(directions) + len(tables)),
        out_specs=tuple(specs(0, 2)),
        scratch_shapes=[
            pltpu.VMEM((2, TILES, LANES), jnp.float32),
            pltpu.VMEM((4 * SPAN, BLOCKS * LANES), jnp.bfloat16),
            pltpu.VMEM((TILES, 4 * LANES), jnp.bfloat16),
            pltpu.VMEM((TILES, 4 * LANES), jnp.bfloat16),
            pltpu.VMEM((4 * SPAN, BLOCKS * LANES), jnp.bfloat16),
            pltpu.VMEM((2 * SPAN, BLOCKS * LANES), jnp.float32),
            pltpu.VMEM((2, TILES, LANES), jnp.float32),
        ],
        compiler_params=limit(20),
        cost_estimate=pl.CostEstimate(
            flops=12 * segments * TILES * 6 * LANES * 4 * LANES,
            transcendentals=0,
            bytes_accessed=4 * segments * 4 * TILES * LANES,
        ),
        name="apply_normal",
    )(core, *steps, *directions, *tables)


def swap_cores(value):
    return lax.ppermute(value, "core", [(0, 1), (1, 0)])


def exchange(value, axes):
    return lax.all_to_all(value, axes, 0, 0, tiled=True)


def share(parts, count, copies):
    rows = parts.shape[0] // count
    shared = pl.pallas_call(
        share_kernel,
        out_shape=jax.ShapeDtypeStruct((copies, rows, LANES), jnp.float32),
        in_specs=specs(0, 1),
        out_specs=specs(0, 1)[0],
        compiler_params=limit(2),
        name="sum_and_copy",
    )(parts.reshape(count, rows, LANES))
    return shared.reshape(copies * rows, LANES)


def sum_to_owners(keep, send):
    return exchange(keep + swap_cores(send), SAME_CORE)


def sum_for_all(keep, send):
    copies = share(exchange(keep + swap_cores(send), ("y", "x")), 16, 8)
    copies = share(exchange(copies, ("z_lo", "z_hi")), 8, 16)
    mine = exchange(copies, ("y", "x"))
    return mine, swap_cores(mine)


def update(step_alpha, step_beta, parts, right_side, own_sum):
    own = jax.ShapeDtypeStruct(right_side.shape, jnp.float32)
    return pl.pallas_call(
        update_kernel,
        out_shape=(own, own),
        in_specs=specs(2, 3),
        out_specs=tuple(specs(0, 2)),
        compiler_params=limit(2),
        name="last_update",
    )(step_alpha, step_beta, parts.reshape(-1, 2 * right_side.shape[0], LANES), right_side, own_sum)


def shards(
    right_side, sensitivity, field_map, seg_map, sample_rows, density, step_alpha, step_beta
):
    seg_local = sample_rows.shape[0]
    first_segment = lax.axis_index(("y", "core")) * seg_local
    core = lax.axis_index("core").reshape(1)
    mine = exchange(jnp.tile(right_side, (DEVICES // 2, 1)), SAME_CORE)
    tables, core = prepare(
        first_segment.reshape(1),
        core,
        sensitivity,
        field_map.T,
        seg_map.T,
        sample_rows,
        jnp.swapaxes(density, 1, 2),
    )
    mine, core = lax.optimization_barrier((mine, core))
    gathered = (mine, swap_cores(mine))
    tables = (tables, jnp.asarray(transform_constants()))
    sums = sum_for_all(*apply_normal(core, (), gathered, tables))
    own_tiles = right_side.shape[0]
    own_start = lax.axis_index(SAME_CORE) * own_tiles
    own_sum = lax.dynamic_slice_in_dim(sums[0], own_start, own_tiles, 0)
    parts = sum_to_owners(
        *apply_normal(core, (step_alpha, step_beta), (*gathered, *sums), tables)
    )
    return update(step_alpha, step_beta, parts, right_side, own_sum)


def solution(mesh):
    axes = ("y", "core", "x", "z_lo", "z_hi")
    fine_mesh = jax.sharding.Mesh(mesh.devices.reshape(4, 2, 4, 4, 2), axes)
    seg, coil, tile = ("y", "core"), ("x", "z_lo"), "z_hi"
    placed = (
        P(axes, None),
        P(coil, None, None),
        P(),
        P(),
        P(seg, tile),
        P(seg, tile, None),
        P(),
        P(),
    )
    return jax.shard_map(
        shards,
        mesh=fine_mesh,
        in_specs=placed,
        out_specs=(P(axes, None), P(axes, None)),
        check_vma=False,
    )
```
